512 devices in a mesh: ctx: 64 (over y, z), head: 8 (over x, core).
Axes of the slice: x: 4, y: 8, z: 8, core: 2. Of those that a mesh axis runs over, the one named last changes fastest.
Arguments:
- probe_matrix: bfloat16 [32768, 4096], P('ctx', 'head'), may hold values from -6 to 6
- lookup_matrix: bfloat16 [32768, 4096], P('ctx', 'head'), may hold values from -6 to 6
- content_matrix: bfloat16 [32768, 4096], P('ctx', 'head'), may hold values from -6 to 6
- log_retention: float32 [32, 32768], P('head', 'ctx'), may hold values from -1.5 to 0
- following_observation_vector: bfloat16 [32768, 4096], P('ctx', 'head'), may hold values from -6 to 6
- rescaler_coefficients: float32 [4096], P('head'), may hold values from 0.25 to 1.75
- payoff_objective_coefficient: float32 [32768], P('ctx'), may hold values from 0.1 to 4
Outputs:
- surprise_payoff: float32 [32768], P('ctx')
- grad_queries: bfloat16 [32768, 4096], P('ctx', 'head')
- grad_keys: bfloat16 [32768, 4096], P('ctx', 'head')
- grad_values: bfloat16 [32768, 4096], P('ctx', 'head')
- scaling_derivative_mean: float32 [4096], P('head')
The draws below stay inside these ranges and needn't reach their ends.
All inputs are finite; a program needn't handle non-finite values.
Results may differ from the reference program's by a relative error of at most 0.0095.
Values may be sent and summed in bfloat16 or wider, within the bound.
No kernel may reach another device: no remote copies, remote signals or barrier semaphores. Data moves between devices by JAX's collectives and lax.ppermute only.
A program may use at most 64 MiB of HBM per device.

```python
import math
import jax
import jax.numpy as jnp
from jax import lax

ATTENTION_HEADS = 32
HEAD_DIM = 128
TOK_DEV = 512
HIDDEN_DIMENSION = 4096
EPISODE_STEPS = 32768


def draw_log_retention(key, part):
    lookup_matrix = jax.random.split(jax.random.fold_in(key, 11), 6)
    slow_share = 0.5
    slow = jax.random.uniform(lookup_matrix[0], (ATTENTION_HEADS,), jnp.float32) < slow_share
    fast_rate = jnp.exp(jax.random.uniform(lookup_matrix[1], (ATTENTION_HEADS,), jnp.float32, math.log(1.0 / 50.0), math.log(1.0 / 30.0)))
    slow_rate = 0.6 / EPISODE_STEPS
    decay_rate = jnp.where(slow, slow_rate, fast_rate)
    blocks = EPISODE_STEPS // TOK_DEV
    block_multiplier = jnp.exp(jax.random.uniform(lookup_matrix[2], (ATTENTION_HEADS, blocks), jnp.float32, math.log(0.5), math.log(2.0)))
    block_multiplier = jnp.repeat(block_multiplier, TOK_DEV, axis=1)
    coarse_estimate = jax.random.uniform(lookup_matrix[3], (ATTENTION_HEADS, EPISODE_STEPS), jnp.float32, 0.5, 1.5)
    group_location = jax.random.randint(lookup_matrix[4], (ATTENTION_HEADS, 3), 0, EPISODE_STEPS)
    group_size = jnp.log(jax.random.uniform(lookup_matrix[5], (ATTENTION_HEADS, 3), jnp.float32, 0.5, 0.8))
    token_position = jnp.arange(EPISODE_STEPS, dtype=jnp.int32)
    token_groups = jnp.sum(jnp.where(token_position[None, None, :] == group_location[:, :, None], group_size[:, :, None], 0.0), axis=1)
    return -decay_rate[:, None] * block_multiplier * coarse_estimate + token_groups


def draw_payoff_objective_coefficient(key, part):
    lookup_matrix = jax.random.split(jax.random.fold_in(key, 23), 2)
    token_position = jnp.arange(EPISODE_STEPS, dtype=jnp.float32)
    ramp = 0.5 + 1.5 * token_position / (EPISODE_STEPS - 1)
    coarse_estimate = jax.random.uniform(lookup_matrix[1], (EPISODE_STEPS,), jnp.float32, 0.5, 1.5)
    return ramp * coarse_estimate


def level_of(own_key, shape, cuts, low, largest):
    def one(dim, blocks):
        heights = jax.random.uniform(jax.random.fold_in(jax.random.fold_in(own_key, 6), dim), (blocks,), jnp.float32, low / len(cuts), largest / len(cuts))
        return jnp.repeat(jnp.exp(heights), shape[dim] // blocks).reshape((-1,) + (1,) * (len(shape) - dim - 1))

    factor_of = one(*cuts[0])
    for cut in cuts[1:]:
        factor_of = factor_of * one(*cut)
    return factor_of


def normal_values(key, extent, deviation, most, shards=(), kind=jnp.bfloat16):
    values = jax.random.normal(key, extent, jnp.float32) * deviation
    if len(shards) > 0:
        values = level_of(key, extent, shards, -0.22, 0.18) * values
    return jnp.clip(values, min=-most, max=most).astype(kind)


def setup_inputs(seed: int = 0) -> dict:
    streams_of = jax.random.split(jax.random.key(seed), 8)
    return {
        "probe_matrix": normal_values(streams_of[0], (EPISODE_STEPS, HIDDEN_DIMENSION), 1.0, 6.0, ((0, 64), (1, 8))),
        "lookup_matrix": normal_values(streams_of[1], (EPISODE_STEPS, HIDDEN_DIMENSION), 1.0, 6.0, ((0, 64), (1, 8))),
        "content_matrix": normal_values(streams_of[2], (EPISODE_STEPS, HIDDEN_DIMENSION), 1.0, 6.0, ((0, 64), (1, 8))),
        "log_retention": draw_log_retention(jax.random.fold_in(streams_of[7], 71), 0),
        "following_observation_vector": normal_values(streams_of[4], (EPISODE_STEPS, HIDDEN_DIMENSION), 1.0, 6.0, ((0, 64), (1, 8))),
        "rescaler_coefficients": jnp.clip(1.0 + 0.15 * jax.random.normal(streams_of[5], (HIDDEN_DIMENSION,), jnp.float32), 0.25, 1.75),
        "payoff_objective_coefficient": draw_payoff_objective_coefficient(jax.random.fold_in(streams_of[7], 71), 0),
    }


EPS = 1e-06

def product(form, left, right):
    return jnp.einsum(form, left.astype(jnp.float32), right.astype(jnp.float32))

def block_parts(query_block, key_block, forget_block):
    cumulative = jnp.cumsum(forget_block, axis=1)
    count = forget_block.shape[1]
    token_position = jnp.arange(count, dtype=jnp.int32)
    causal = (token_position[:, None] >= token_position[None, :])[None]
    gaps = cumulative[:, :, None] - cumulative[:, None, :]
    decays = jnp.where(causal, jnp.exp(jnp.where(causal, gaps, jnp.float32(0.0))), jnp.float32(0.0))
    attn_scale = HEAD_DIM ** (-0.5)
    probs = (product('thd,shd->hts', query_block, key_block) * attn_scale * decays).astype(jnp.bfloat16)
    start_decay = jnp.exp(cumulative).T
    total = cumulative[:, -1]
    tail_decay = jnp.exp(total[:, None] - cumulative).T
    return (decays, probs, start_decay, total, tail_decay)

def forward_step(state, inputs):
    query_block, key_block, value_block, forget_block = inputs
    decays, probs, start_decay, total, tail_decay = block_parts(query_block, key_block, forget_block)
    attn_scale = HEAD_DIM ** (-0.5)
    local_part = product('hts,shd->thd', probs, value_block)
    state_low = state.astype(jnp.bfloat16)
    carried = product('thd,hde->the', query_block, state_low)
    attn_out = local_part + attn_scale * start_decay[:, :, None] * carried
    key_decayed = (key_block.astype(jnp.float32) * tail_decay[:, :, None]).astype(jnp.bfloat16)
    summary = product('shd,she->hde', key_decayed, value_block)
    new_state = jnp.exp(total)[:, None, None] * state + summary
    return (new_state, (attn_out, state_low))

def backward_step(state, inputs):
    query_block, key_block, value_block, forget_block, state_low, grad_out = inputs
    decays, probs, start_decay, total, tail_decay = block_parts(query_block, key_block, forget_block)
    attn_scale = HEAD_DIM ** (-0.5)
    later_low = state.astype(jnp.bfloat16)
    grad_probs = (product('the,she->hts', grad_out, value_block) * attn_scale * decays).astype(jnp.bfloat16)
    probe_derivative = product('hts,shd->thd', grad_probs, key_block) + attn_scale * start_decay[:, :, None] * product('the,hde->thd', grad_out, state_low)
    lookup_derivative = product('hts,thd->shd', grad_probs, query_block) + tail_decay[:, :, None] * product('she,hde->shd', value_block, later_low)
    content_derivative = product('hts,the->she', probs, grad_out) + tail_decay[:, :, None] * product('shd,hde->she', key_block, later_low)
    query_decayed = (query_block.astype(jnp.float32) * (attn_scale * start_decay)[:, :, None]).astype(jnp.bfloat16)
    back_summary = product('thd,the->hde', query_decayed, grad_out)
    new_state = back_summary + jnp.exp(total)[:, None, None] * state
    return (new_state, (probe_derivative.astype(jnp.bfloat16), lookup_derivative.astype(jnp.bfloat16), content_derivative.astype(jnp.bfloat16)))

def reference(probe_matrix, lookup_matrix, content_matrix, log_retention, following_observation_vector, rescaler_coefficients, payoff_objective_coefficient):
    blocks = EPISODE_STEPS // TOK_DEV

    def split(array):
        return array.reshape(blocks, TOK_DEV, ATTENTION_HEADS, HEAD_DIM)
    forget_blocks = log_retention.reshape(ATTENTION_HEADS, blocks, TOK_DEV).transpose(1, 0, 2)
    initial = jnp.zeros((ATTENTION_HEADS, HEAD_DIM, HEAD_DIM), jnp.float32)
    final_state, outputs = lax.scan(forward_step, initial, (split(probe_matrix), split(lookup_matrix), split(content_matrix), forget_blocks))
    attn_out, states = outputs
    output_flat = attn_out.reshape(EPISODE_STEPS, HIDDEN_DIMENSION)
    rms = jnp.sqrt(lax.optimization_barrier(jnp.sum(output_flat * output_flat, axis=1)) / HIDDEN_DIMENSION + EPS)
    rescaled_activations = output_flat / rms[:, None]
    predicted_minus_actual = rescaler_coefficients[None, :] * rescaled_activations - following_observation_vector.astype(jnp.float32)
    surprise_payoff = lax.optimization_barrier(jnp.sum(predicted_minus_actual * predicted_minus_actual, axis=1)) / HIDDEN_DIMENSION
    discrepancy_adjoint = payoff_objective_coefficient[:, None] * predicted_minus_actual
    normalized_adjoint = discrepancy_adjoint * rescaler_coefficients[None, :]
    inner_accumulation = lax.optimization_barrier(jnp.sum(normalized_adjoint * rescaled_activations, axis=1))
    grad_out = ((normalized_adjoint - rescaled_activations * (inner_accumulation / HIDDEN_DIMENSION)[:, None]) / rms[:, None]).astype(jnp.bfloat16)
    scaling_derivative_mean = lax.optimization_barrier(jnp.sum(discrepancy_adjoint * rescaled_activations, axis=0)) / EPISODE_STEPS
    first_state, grads = lax.scan(backward_step, initial, (split(probe_matrix), split(lookup_matrix), split(content_matrix), forget_blocks, states, split(grad_out)), reverse=True)
    probe_derivative, lookup_derivative, content_derivative = grads
    return (surprise_payoff, probe_derivative.reshape(EPISODE_STEPS, HIDDEN_DIMENSION), lookup_derivative.reshape(EPISODE_STEPS, HIDDEN_DIMENSION), content_derivative.reshape(EPISODE_STEPS, HIDDEN_DIMENSION), scaling_derivative_mean)
```

```python
import jax
import jax.numpy as jnp
from jax import lax
from jax.experimental import pallas as pl
from jax.experimental.pallas import tpu as pltpu
from jax.sharding import PartitionSpec as P

HEAD_DIM = 128
HIDDEN_DIMENSION = 4096
EPS = 1e-06
SCALE = HEAD_DIM ** (-0.5)
TOK = 512
HEADS = 4
BLOCKS = 64
PER_HEAD = BLOCKS // HEADS
HALF = TOK // 2
FAR = -1e9

F32 = jnp.float32
BF16 = jnp.bfloat16

NN = (((1,), (0,)), ((), ()))
NT = (((1,), (1,)), ((), ()))
TN = (((0,), (0,)), ((), ()))


def mm(a, b, dims=NN):
    return lax.dot_general(a, b, dims, preferred_element_type=F32)


def head(h):
    return slice(h * HEAD_DIM, (h + 1) * HEAD_DIM)


def pieces(x):
    hi = x.astype(BF16).astype(F32)
    rest = x - hi
    mid = rest.astype(BF16).astype(F32)
    return hi, mid, rest - mid


def aux_tile(row):
    hi, mid, lo = pieces(row)
    at = lax.broadcasted_iota(jnp.int32, (8, HEAD_DIM), 0)
    return jnp.where(at == 0, hi, jnp.where(at == 1, mid, jnp.where(at == 2, lo, 0.0)))


def message(matrix, row):
    data = matrix.reshape(PER_HEAD, 8, HEAD_DIM)
    aux = jnp.broadcast_to(aux_tile(row)[None], (PER_HEAD, 8, HEAD_DIM))
    return jnp.concatenate([data, aux], axis=1).astype(BF16)


def summary_kernel(retention, keys, values, out, cum_out):
    rows = jnp.concatenate([retention[...], jnp.zeros((8 - HEADS, TOK), F32)], axis=0)
    parts = pieces(rows)
    stacked = jnp.concatenate(
        [p[:, c * 128 : (c + 1) * 128] for c in range(TOK // 128) for p in parts], axis=0
    ).astype(BF16)
    first = lax.broadcasted_iota(jnp.int32, (128, 128), 0)
    second = lax.broadcasted_iota(jnp.int32, (128, 128), 1)
    upper = jnp.where(first <= second, 1.0, 0.0).astype(BF16)
    sums = mm(stacked, upper)
    offset = jnp.zeros((8, 1), F32)
    chunks = []
    for c in range(TOK // 128):
        own = sums[24 * c : 24 * c + 8] + sums[24 * c + 8 : 24 * c + 16] + sums[24 * c + 16 : 24 * c + 24]
        own = own + offset
        offset = own[:, 127:128]
        chunks.append(own)
    cum = jnp.concatenate(chunks, axis=1)
    cum_out[...] = cum
    tail = jnp.exp(offset - cum)
    decay = jnp.broadcast_to(jnp.exp(offset), (8, HEAD_DIM))
    for h in range(HEADS):
        turned = keys[:, head(h)].T
        key_decayed = (turned.astype(F32) * tail[h : h + 1]).astype(BF16)
        out[h * PER_HEAD : (h + 1) * PER_HEAD] = message(
            mm(key_decayed, values[:, head(h)]), decay[h : h + 1]
        )


def decay_rows(aux):
    return jnp.broadcast_to(aux[0:1] + aux[1:2] + aux[2:3], (8, HEAD_DIM))


def forward_scan_kernel(arrived, out):
    state = jnp.zeros((8, HEAD_DIM), F32)
    for pair in range(BLOCKS // 2):
        both = []
        for b in (2 * pair, 2 * pair + 1):
            both.append(state)
            got = arrived[b].astype(F32)
            state = decay_rows(got[8:16]) * state + got[0:8]
        out[16 * pair : 16 * pair + 16] = jnp.concatenate(both, axis=0).astype(BF16)


def backward_scan_kernel(arrived, decays, out):
    gain = jnp.zeros((8, HEAD_DIM), F32)
    for b in range(BLOCKS):
        gain = gain + arrived[b].astype(F32)[8:16]
    aux = aux_tile(gain[0:1] + gain[1:2] + gain[2:3])
    state = jnp.zeros((8, HEAD_DIM), F32)
    for b in reversed(range(BLOCKS)):
        out[b] = jnp.concatenate([state, aux], axis=0).astype(BF16)
        state = decay_rows(decays[b].astype(F32)[8:16]) * state + arrived[b].astype(F32)[0:8]


def block_decay(cum, columns, h, i):
    rows, width = slice(i * HALF, (i + 1) * HALF), (i + 1) * HALF
    gap = columns[rows, h : h + 1] - cum[h : h + 1, 0:width]
    t = lax.broadcasted_iota(jnp.int32, (HALF, width), 0) + i * HALF
    s = lax.broadcasted_iota(jnp.int32, (HALF, width), 1)
    return jnp.exp(jnp.where(s <= t, gap, FAR))


def local_kernel(queries, keys, values, target, cum, local, probs, turned, columns, target_square):
    total = cum[:, TOK - 1 : TOK]
    start = jnp.exp(cum[...]) * SCALE
    tail = jnp.exp(total - cum[...])
    side = jnp.concatenate([cum[...], start, tail, jnp.zeros((104, TOK), F32)], axis=0).T
    columns[...] = side
    square = jnp.zeros((TOK, HEAD_DIM), F32)
    for h in range(HEADS):
        x = target[:, head(h)].astype(F32)
        square = square + x * x
        q, k, v = queries[:, head(h)], keys[:, head(h)], values[:, head(h)]
        turned[head(h), :] = (q.T.astype(F32) * start[h : h + 1]).astype(BF16)
        for i in range(2):
            rows, width = slice(i * HALF, (i + 1) * HALF), (i + 1) * HALF
            scores = mm(q[rows], k[0:width], NT)
            p = (scores * SCALE * block_decay(cum, side, h, i)).astype(BF16)
            probs[h, rows, 0:width] = p
            local[rows, head(h)] = mm(p, v[0:width])
    target_square[...] = jnp.sum(square.T, axis=0, keepdims=True)


def output_kernel(queries, states, local, columns, target, gain, target_square, attn, sums):
    square = jnp.zeros((TOK, HEAD_DIM), F32)
    gain_square = square
    cross = square
    for h in range(HEADS):
        carried = mm(queries[:, head(h)], states[head(h), :])
        o = local[:, head(h)] + columns[:, 8 + h : 9 + h] * carried
        attn[:, head(h)] = o
        gained = gain[:, head(h)] * o
        square = square + o * o
        gain_square = gain_square + gained * gained
        cross = cross + gained * target[:, head(h)].astype(F32)
    four = jnp.concatenate(
        [jnp.sum(a.T, axis=0, keepdims=True) for a in (square, gain_square, cross)]
        + [target_square[...]],
        axis=0,
    )
    for d in range(8):
        sums[d] = four


def gradient_kernel(sums, attn, target, gain, weight, turned, out, grad_out, payoff):
    four = jnp.sum(sums[...], axis=0)
    mean_square = four[0:1] / HIDDEN_DIMENSION + EPS
    inverse = 1.0 / jnp.sqrt(mean_square)
    pred_square = four[1:2] / mean_square
    pred_cross = four[2:3] * inverse
    payoff[...] = (pred_square - 2.0 * pred_cross + four[3:4]) / HIDDEN_DIMENSION
    inner = weight[...] * (pred_square - pred_cross)
    a = weight[...] / mean_square
    b = weight[...] * inverse
    c = inner / (HIDDEN_DIMENSION * mean_square)
    side = jnp.concatenate([a, b, c, jnp.zeros((125, TOK), F32)], axis=0).T
    a, b, c = side[:, 0:1], side[:, 1:2], side[:, 2:3]
    for h in range(HEADS):
        o, x, g = attn[:, head(h)], target[:, head(h)].astype(F32), gain[:, head(h)]
        error = a * (g * o) - b * x
        gain_row = jnp.sum(error * o, axis=0, keepdims=True)
        d = (error * g - c * o).astype(BF16)
        grad_out[:, head(h)] = d
        out[h * PER_HEAD : (h + 1) * PER_HEAD] = message(mm(turned[head(h), :], d), gain_row)


def local_gradient_kernel(
    grad_out, queries, keys, values, probs, states, cum, columns, grad_q, local_k, local_v
):
    for h in range(HEADS):
        q, k, v, d = queries[:, head(h)], keys[:, head(h)], values[:, head(h)], grad_out[:, head(h)]
        carried = columns[:, 8 + h : 9 + h] * mm(d, states[head(h), :], NT)
        parts = []
        for i in range(2):
            rows, width = slice(i * HALF, (i + 1) * HALF), (i + 1) * HALF
            grads = mm(d[rows], v[0:width], NT)
            gp = (grads * SCALE * block_decay(cum, columns, h, i)).astype(BF16)
            parts.append(gp)
            grad_q[rows, head(h)] = (mm(gp, k[0:width]) + carried[rows]).astype(BF16)
        early = jnp.concatenate([parts[0], parts[1][:, 0:HALF]], axis=0)
        local_k[0:HALF, head(h)] = mm(early, q, TN)
        local_k[HALF:TOK, head(h)] = mm(parts[1][:, HALF:TOK], q[HALF:TOK], TN)
        local_v[0:HALF, head(h)] = mm(probs[h, :, 0:HALF], d, TN)
        local_v[HALF:TOK, head(h)] = mm(probs[h, HALF:TOK, HALF:TOK], d[HALF:TOK], TN)


def final_kernel(arrived, keys, values, local_k, local_v, columns, grad_k, grad_v, gain_out):
    for h in range(HEADS):
        got = arrived[h * PER_HEAD : (h + 1) * PER_HEAD].astype(F32)
        state = got[:, 0:8].reshape(HEAD_DIM, HEAD_DIM).astype(BF16)
        aux = got[0, 8:16]
        gain_out[:, head(h)] = (aux[0:1] + aux[1:2] + aux[2:3]) / (BLOCKS * TOK)
        tail = columns[:, 16 + h : 17 + h]
        grad_k[:, head(h)] = (
            local_k[:, head(h)] + tail * mm(values[:, head(h)], state, NT)
        ).astype(BF16)
        grad_v[:, head(h)] = (
            local_v[:, head(h)] + tail * mm(keys[:, head(h)], state)
        ).astype(BF16)


def call(kernel, outs, args, flops, name):
    moved = sum(a.size * a.dtype.itemsize for a in args)
    moved += sum(o.size * o.dtype.itemsize for o in outs)
    whole = pl.BlockSpec(memory_space=pltpu.VMEM)
    return pl.pallas_call(
        kernel,
        out_shape=outs,
        in_specs=[whole] * len(args),
        out_specs=[whole] * len(outs),
        compiler_params=pltpu.CompilerParams(vmem_limit_bytes=32 * 2**20),
        cost_estimate=pl.CostEstimate(flops=flops, bytes_accessed=moved, transcendentals=0),
        name=name,
    )(*args)


def shape(dims, kind):
    return jax.ShapeDtypeStruct(dims, kind)


def exchange(x, axis):
    return lax.all_to_all(x, axis, 0, 0, tiled=True)


def local_part(queries, keys, values, retention, target, gain, weight):
    wide = TOK * TOK * HEAD_DIM * 2 * HEADS
    narrow = TOK * HEAD_DIM * HEAD_DIM * 2 * HEADS
    gain = gain.reshape(1, -1)
    weight = weight.reshape(1, -1)
    slices = shape((BLOCKS, 16, HEAD_DIM), BF16)
    full32 = shape((TOK, TOK), F32)
    full16 = shape((TOK, TOK), BF16)
    row = shape((1, TOK), F32)

    sent, cum = call(
        summary_kernel, [slices, shape((8, TOK), F32)], [retention, keys, values], narrow, "summary"
    )
    arrived = exchange(sent, "ctx")
    local, probs, turned, columns, target_square = call(
        local_kernel,
        [full32, shape((HEADS, TOK, TOK), BF16), full16, shape((TOK, 128), F32), row],
        [queries, keys, values, target, cum],
        2 * wide,
        "local",
    )
    [back] = call(forward_scan_kernel, [shape((TOK, HEAD_DIM), BF16)], [arrived], 1000, "forward_scan")
    states = exchange(back.reshape(BLOCKS, 8, HEAD_DIM), "ctx").reshape(TOK, HEAD_DIM)
    attn, sums = call(
        output_kernel,
        [full32, shape((8, 4, TOK), F32)],
        [queries, states, local, columns, target, gain, target_square],
        narrow,
        "output",
    )
    sums = exchange(sums, "head")
    sent, grad_out, payoff = call(
        gradient_kernel, [slices, full16, row], [sums, attn, target, gain, weight, turned], narrow, "gradient"
    )
    arrived_back = exchange(sent, "ctx")
    grad_q, local_k, local_v = call(
        local_gradient_kernel,
        [full16, full32, full32],
        [grad_out, queries, keys, values, probs, states, cum, columns],
        4 * wide,
        "local_gradient",
    )
    [back] = call(backward_scan_kernel, [slices], [arrived_back, arrived], 1000, "backward_scan")
    last = exchange(back, "ctx")
    grad_k, grad_v, gain_out = call(
        final_kernel,
        [full16, full16, row],
        [last, keys, values, local_k, local_v, columns],
        2 * narrow,
        "final",
    )
    return payoff.reshape(-1), grad_q, grad_k, grad_v, gain_out.reshape(-1)


def solution(mesh):
    placed = (
        P("ctx", "head"),
        P("ctx", "head"),
        P("ctx", "head"),
        P("head", "ctx"),
        P("ctx", "head"),
        P("head"),
        P("ctx"),
    )
    return jax.shard_map(
        local_part,
        mesh=mesh,
        in_specs=placed,
        out_specs=(P("ctx"), P("ctx", "head"), P("ctx", "head"), P("ctx", "head"), P("head")),
        check_vma=False,
    )
```

```python
import jax
import jax.numpy as jnp
from jax import lax
from jax.experimental import pallas as pl
from jax.experimental.pallas import tpu as pltpu
from jax.sharding import PartitionSpec as P

HEAD_DIM = 128
HIDDEN_DIMENSION = 4096
EPS = 1e-06
SCALE = HEAD_DIM ** (-0.5)
TOK = 512
HEADS = 4
BLOCKS = 64
PER_HEAD = BLOCKS // HEADS
HALF = TOK // 2
FAR = -1e9

F32 = jnp.float32
BF16 = jnp.bfloat16

NN = (((1,), (0,)), ((), ()))
NT = (((1,), (1,)), ((), ()))
TN = (((0,), (0,)), ((), ()))


def mm(a, b, dims=NN):
    return lax.dot_general(a, b, dims, preferred_element_type=F32)


def head(h):
    return slice(h * HEAD_DIM, (h + 1) * HEAD_DIM)


def pieces(x):
    hi = x.astype(BF16).astype(F32)
    rest = x - hi
    mid = rest.astype(BF16).astype(F32)
    return hi, mid, rest - mid


def fetch(source, target, sems, base):
    copies = []
    for h in range(HEADS):
        copy = pltpu.make_async_copy(
            source.at[:, head(h)], target.at[:, head(h)], sems.at[base + h]
        )
        copy.start()
        copies.append(copy)
    return copies


def aux_tile(row):
    hi, mid, lo = pieces(row)
    at = lax.broadcasted_iota(jnp.int32, (8, HEAD_DIM), 0)
    return jnp.where(at == 0, hi, jnp.where(at == 1, mid, jnp.where(at == 2, lo, 0.0)))


def message(matrix, tile):
    data = matrix.reshape(PER_HEAD, 8, HEAD_DIM)
    aux = jnp.broadcast_to(tile[None], (PER_HEAD, 8, HEAD_DIM))
    return jnp.concatenate([data, aux], axis=1).astype(BF16)


def summary_kernel(
    retention_far, keys_far, values_far, out, cum_out, keys, values, sems, retention, retention_sem
):
    got_retention = pltpu.make_async_copy(retention_far, retention, retention_sem)
    got_retention.start()
    got_keys = fetch(keys_far, keys, sems, 0)
    got_values = fetch(values_far, values, sems, HEADS)
    got_retention.wait()
    rows = jnp.concatenate([retention[...], jnp.zeros((8 - HEADS, TOK), F32)], axis=0)
    parts = pieces(rows)
    stacked = jnp.concatenate(
        [p[:, c * 128 : (c + 1) * 128] for c in range(TOK // 128) for p in parts], axis=0
    ).astype(BF16)
    first = lax.broadcasted_iota(jnp.int32, (128, 128), 0)
    second = lax.broadcasted_iota(jnp.int32, (128, 128), 1)
    upper = jnp.where(first <= second, 1.0, 0.0).astype(BF16)
    sums = mm(stacked, upper)
    offset = jnp.zeros((8, 1), F32)
    chunks = []
    for c in range(TOK // 128):
        own = sums[24 * c : 24 * c + 8] + sums[24 * c + 8 : 24 * c + 16] + sums[24 * c + 16 : 24 * c + 24]
        own = own + offset
        offset = own[:, 127:128]
        chunks.append(own)
    cum = jnp.concatenate(chunks, axis=1)
    cum_out[...] = cum
    tail = jnp.exp(offset - cum)
    decay = jnp.broadcast_to(jnp.exp(offset), (8, HEAD_DIM))
    for h in range(HEADS):
        got_keys[h].wait()
        turned = keys[:, head(h)].T
        key_decayed = (turned.astype(F32) * tail[h : h + 1]).astype(BF16)
        got_values[h].wait()
        out[h * PER_HEAD : (h + 1) * PER_HEAD] = message(
            mm(key_decayed, values[:, head(h)]), aux_tile(decay[h : h + 1])
        )


def decay_rows(aux):
    return jnp.broadcast_to(aux[0:1] + aux[1:2] + aux[2:3], (8, HEAD_DIM))


def forward_scan_kernel(arrived, out):
    state = jnp.zeros((8, HEAD_DIM), F32)
    for pair in range(BLOCKS // 2):
        both = []
        for b in (2 * pair, 2 * pair + 1):
            both.append(state)
            got = arrived[b].astype(F32)
            state = decay_rows(got[8:16]) * state + got[0:8]
        out[16 * pair : 16 * pair + 16] = jnp.concatenate(both, axis=0).astype(BF16)


def backward_scan_kernel(arrived, decays, out):
    state = jnp.zeros((8, HEAD_DIM), F32)
    for pair in reversed(range(BLOCKS // 2)):
        both = []
        for b in (2 * pair + 1, 2 * pair):
            both.append(state)
            state = decay_rows(decays[b].astype(F32)[8:16]) * state + arrived[b].astype(F32)[0:8]
        out[16 * pair : 16 * pair + 16] = jnp.concatenate(both[::-1], axis=0).astype(BF16)


def block_decay(cum, columns, h, i):
    rows, width = slice(i * HALF, (i + 1) * HALF), (i + 1) * HALF
    gap = columns[rows, h : h + 1] - cum[h : h + 1, 0:width]
    t = lax.broadcasted_iota(jnp.int32, (HALF, width), 0) + i * HALF
    s = lax.broadcasted_iota(jnp.int32, (HALF, width), 1)
    return jnp.exp(jnp.where(s <= t, gap, FAR))


def local_kernel(
    queries, keys_far, values_far, target, cum, gain, weight,
    local, turned, columns, rows_out, keys, values, sems,
):
    got_keys = fetch(keys_far, keys, sems, 0)
    got_values = fetch(values_far, values, sems, HEADS)
    total = cum[:, TOK - 1 : TOK]
    start = jnp.exp(cum[...]) * SCALE
    tail = jnp.exp(total - cum[...])
    side = jnp.concatenate([cum[...], start, tail, jnp.zeros((104, TOK), F32)], axis=0).T
    columns[...] = side
    square = jnp.zeros((TOK, HEAD_DIM), F32)
    for h in range(HEADS):
        x = target[:, head(h)].astype(F32)
        square = square + x * x
        got_keys[h].wait()
        got_values[h].wait()
        q, k, v = queries[:, head(h)], keys[:, head(h)], values[:, head(h)]
        turned[head(h), :] = (q.T.astype(F32) * start[h : h + 1]).astype(BF16)
        for i in range(2):
            rows, width = slice(i * HALF, (i + 1) * HALF), (i + 1) * HALF
            scores = mm(q[rows], k[0:width], NT)
            p = (scores * SCALE * block_decay(cum, side, h, i)).astype(BF16)
            local[rows, head(h)] = mm(p, v[0:width])
    rows_out[...] = jnp.concatenate(
        [gain[...], weight[...], jnp.sum(square.T, axis=0, keepdims=True), jnp.zeros((5, TOK), F32)],
        axis=0,
    )


def output_kernel(queries, states, local, columns, target, rows, attn, sums):
    square = jnp.zeros((TOK, HEAD_DIM), F32)
    gain_square = square
    cross = square
    for h in range(HEADS):
        carried = mm(queries[:, head(h)], states[head(h), :])
        o = local[:, head(h)] + columns[:, 8 + h : 9 + h] * carried
        attn[:, head(h)] = o
        gained = rows[0:1, head(h)] * o
        square = square + o * o
        gain_square = gain_square + gained * gained
        cross = cross + gained * target[:, head(h)].astype(F32)
    four = jnp.concatenate(
        [jnp.sum(a.T, axis=0, keepdims=True) for a in (square, gain_square, cross)]
        + [rows[2:3]],
        axis=0,
    )
    for d in range(8):
        sums[d] = four


def gradient_kernel(sums, attn, target, rows, turned, out, grad_out):
    weight = rows[1:2]
    four = jnp.sum(sums[...], axis=0)
    mean_square = four[0:1] / HIDDEN_DIMENSION + EPS
    inverse = 1.0 / jnp.sqrt(mean_square)
    pred_square = four[1:2] / mean_square
    pred_cross = four[2:3] * inverse
    inner = weight * (pred_square - pred_cross)
    a = weight / mean_square
    b = weight * inverse
    c = inner / (HIDDEN_DIMENSION * mean_square)
    side = jnp.concatenate([a, b, c, jnp.zeros((125, TOK), F32)], axis=0).T
    a, b, c = side[:, 0:1], side[:, 1:2], side[:, 2:3]
    gains, backs = [], []
    for h in range(HEADS):
        o, x, g = attn[:, head(h)], target[:, head(h)].astype(F32), rows[0:1, head(h)]
        error = a * (g * o) - b * x
        gains.append(jnp.sum(error * o, axis=0, keepdims=True))
        d = (error * g - c * o).astype(BF16)
        grad_out[:, head(h)] = d
        backs.append(mm(turned[head(h), :], d))
    gains = jnp.concatenate(gains, axis=0)
    high = gains.astype(BF16).astype(F32)
    tile = jnp.concatenate([high, gains - high], axis=0)
    for h in range(HEADS):
        out[h * PER_HEAD : (h + 1) * PER_HEAD] = message(backs[h], tile)


def local_gradient_kernel(
    grad_out, queries, keys_far, values_far, states, cum, columns, sums, arrived,
    grad_q, local_k, local_v, payoff, gain_out, keys, values, sems,
):
    got_keys = fetch(keys_far, keys, sems, 0)
    got_values = fetch(values_far, values, sems, HEADS)
    four = jnp.sum(sums[...], axis=0)
    mean_square = four[0:1] / HIDDEN_DIMENSION + EPS
    pred_square = four[1:2] / mean_square
    pred_cross = four[2:3] / jnp.sqrt(mean_square)
    payoff[...] = (pred_square - 2.0 * pred_cross + four[3:4]) / HIDDEN_DIMENSION
    gains = jnp.zeros((8, HEAD_DIM), F32)
    for b in range(BLOCKS):
        gains = gains + arrived[b].astype(F32)[8:16]
    gain_out[...] = (gains[0:HEADS] + gains[HEADS : 2 * HEADS]) / (BLOCKS * TOK)
    for h in range(HEADS):
        got_keys[h].wait()
        got_values[h].wait()
        q, k, v, d = queries[:, head(h)], keys[:, head(h)], values[:, head(h)], grad_out[:, head(h)]
        carried = columns[:, 8 + h : 9 + h] * mm(d, states[head(h), :], NT)
        parts, probs = [], []
        for i in range(2):
            rows, width = slice(i * HALF, (i + 1) * HALF), (i + 1) * HALF
            decay = SCALE * block_decay(cum, columns, h, i)
            probs.append((mm(q[rows], k[0:width], NT) * decay).astype(BF16))
            gp = (mm(d[rows], v[0:width], NT) * decay).astype(BF16)
            parts.append(gp)
            grad_q[rows, head(h)] = (mm(gp, k[0:width]) + carried[rows]).astype(BF16)
        for side, near, far in ((local_k, parts, q), (local_v, probs, d)):
            early = jnp.concatenate([near[0], near[1][:, 0:HALF]], axis=0)
            side[0:HALF, head(h)] = mm(early, far, TN).astype(BF16)
            side[HALF:TOK, head(h)] = mm(near[1][:, HALF:TOK], far[HALF:TOK], TN).astype(BF16)


def final_kernel(
    states, keys, values, local_k, local_v, columns, grad_k_far, grad_v_far, grad_k, grad_v, sems
):
    copies = []
    for h in range(HEADS):
        state = states[head(h), :]
        tail = columns[:, 16 + h : 17 + h]
        for i, (near, far, local, moved) in enumerate(
            (
                (grad_k, grad_k_far, local_k, mm(values[:, head(h)], state, NT)),
                (grad_v, grad_v_far, local_v, mm(keys[:, head(h)], state)),
            )
        ):
            near[:, head(h)] = (local[:, head(h)].astype(F32) + tail * moved).astype(BF16)
            copy = pltpu.make_async_copy(
                near.at[:, head(h)], far.at[:, head(h)], sems.at[2 * h + i]
            )
            copy.start()
            copies.append(copy)
    for copy in copies:
        copy.wait()


NEAR = pl.BlockSpec(memory_space=pltpu.VMEM)
FAR_AWAY = pl.BlockSpec(memory_space=pltpu.HBM)


def call(kernel, outs, args, flops, name, far=(), far_outs=(), pairs=False, more=()):
    moved = sum(a.size * a.dtype.itemsize for a in args)
    moved += sum(o.size * o.dtype.itemsize for o in outs)
    scratch = []
    if pairs:
        scratch = [pltpu.VMEM((TOK, TOK), BF16)] * 2 + [pltpu.SemaphoreType.DMA((2 * HEADS,))]
    return pl.pallas_call(
        kernel,
        out_shape=outs,
        in_specs=[FAR_AWAY if i in far else NEAR for i in range(len(args))],
        out_specs=[FAR_AWAY if i in far_outs else NEAR for i in range(len(outs))],
        scratch_shapes=[*scratch, *more],
        compiler_params=pltpu.CompilerParams(vmem_limit_bytes=32 * 2**20),
        cost_estimate=pl.CostEstimate(flops=flops, bytes_accessed=moved, transcendentals=0),
        name=name,
    )(*(pltpu.with_memory_space_constraint(a, pltpu.HBM) if i in far else a for i, a in enumerate(args)))


def shape(dims, kind):
    return jax.ShapeDtypeStruct(dims, kind)


def exchange(x, axis):
    return lax.all_to_all(x, axis, 0, 0, tiled=True)


def local_part(queries, keys, values, retention, target, gain, weight):
    wide = TOK * TOK * HEAD_DIM * 2 * HEADS
    narrow = TOK * HEAD_DIM * HEAD_DIM * 2 * HEADS
    gain = gain.reshape(1, -1)
    weight = weight.reshape(1, -1)
    slices = shape((BLOCKS, 16, HEAD_DIM), BF16)
    full32 = shape((TOK, TOK), F32)
    full16 = shape((TOK, TOK), BF16)
    row = shape((1, TOK), F32)

    sent, cum = call(
        summary_kernel,
        [slices, shape((8, TOK), F32)],
        [retention, keys, values],
        narrow,
        "summary",
        far=(0, 1, 2),
        pairs=True,
        more=[pltpu.VMEM((HEADS, TOK), F32), pltpu.SemaphoreType.DMA],
    )
    arrived = exchange(sent, "ctx")
    local, turned, columns, rows = call(
        local_kernel,
        [full32, full16, shape((TOK, 128), F32), shape((8, TOK), F32)],
        [queries, keys, values, target, cum, gain, weight],
        2 * wide,
        "local",
        far=(1, 2),
        pairs=True,
    )
    back = shape((TOK, HEAD_DIM), BF16)
    [states] = call(forward_scan_kernel, [back], [arrived], 1000, "forward_scan")
    states = exchange(states.reshape(BLOCKS, 8, HEAD_DIM), "ctx").reshape(TOK, HEAD_DIM)
    attn, sums = call(
        output_kernel,
        [full32, shape((8, 4, TOK), F32)],
        [queries, states, local, columns, target, rows],
        narrow,
        "output",
    )
    sums = exchange(sums, "head")
    sent, grad_out = call(
        gradient_kernel, [slices, full16], [sums, attn, target, rows, turned], narrow, "gradient"
    )
    arrived_back = exchange(sent, "ctx")
    grad_q, local_k, local_v, payoff, gain_out = call(
        local_gradient_kernel,
        [full16, full16, full16, row, shape((HEADS, HEAD_DIM), F32)],
        [grad_out, queries, keys, values, states, cum, columns, sums, arrived_back],
        6 * wide,
        "local_gradient",
        far=(2, 3),
        pairs=True,
    )
    [later] = call(backward_scan_kernel, [back], [arrived_back, arrived], 1000, "backward_scan")
    later = exchange(later.reshape(BLOCKS, 8, HEAD_DIM), "ctx").reshape(TOK, HEAD_DIM)
    grad_k, grad_v = call(
        final_kernel,
        [full16, full16],
        [later, keys, values, local_k, local_v, columns],
        2 * narrow,
        "final",
        far_outs=(0, 1),
        pairs=True,
    )
    return payoff.reshape(-1), grad_q, grad_k, grad_v, gain_out.reshape(-1)


def solution(mesh):
    placed = (
        P("ctx", "head"),
        P("ctx", "head"),
        P("ctx", "head"),
        P("head", "ctx"),
        P("ctx", "head"),
        P("head"),
        P("ctx"),
    )
    return jax.shard_map(
        local_part,
        mesh=mesh,
        in_specs=placed,
        out_specs=(P("ctx"), P("ctx", "head"), P("ctx", "head"), P("ctx", "head"), P("head")),
        check_vma=False,
    )
```

```python
import math

import jax
import jax.numpy as jnp
from jax import lax
from jax.experimental import pallas as pl
from jax.experimental.pallas import tpu as pltpu
from jax.sharding import PartitionSpec as P

HEAD_DIM = 128
HIDDEN_DIMENSION = 4096
EPS = 1e-06
SCALE = HEAD_DIM ** (-0.5)
TOK = 512
HEADS = 4
BLOCKS = 64
PER_HEAD = BLOCKS // HEADS
HALF = TOK // 2
FAR = -1e9
LOG2E = math.log2(math.e)
LOG2_SCALE = math.log2(SCALE)

F32 = jnp.float32
BF16 = jnp.bfloat16

NN = (((1,), (0,)), ((), ()))
NT = (((1,), (1,)), ((), ()))
TN = (((0,), (0,)), ((), ()))


def mm(a, b, dims=NN):
    return lax.dot_general(a, b, dims, preferred_element_type=F32)


def head(h):
    return slice(h * HEAD_DIM, (h + 1) * HEAD_DIM)


def pieces(x):
    hi = x.astype(BF16).astype(F32)
    rest = x - hi
    mid = rest.astype(BF16).astype(F32)
    return hi, mid, rest - mid


def copy(source, target, sem):
    moving = pltpu.make_async_copy(source, target, sem)
    moving.start()
    return moving


def aux_tile(row):
    hi, mid, lo = pieces(row)
    at = lax.broadcasted_iota(jnp.int32, (8, HEAD_DIM), 0)
    return jnp.where(at == 0, hi, jnp.where(at == 1, mid, jnp.where(at == 2, lo, 0.0)))


def message(matrix, tile):
    data = matrix.reshape(PER_HEAD, 8, HEAD_DIM)
    aux = jnp.broadcast_to(tile[None], (PER_HEAD, 8, HEAD_DIM))
    return jnp.concatenate([data, aux], axis=1).astype(BF16)


def summary_kernel(
    retention_far, keys_far, values_far, gain_far, weight_far,
    out, cum_out, keys, values, gain, weight, retention, sems,
):
    got_retention = copy(retention_far, retention, sems.at[0])
    got_keys = copy(keys_far, keys, sems.at[1])
    got_values = copy(values_far, values, sems.at[2])
    got_gain = copy(gain_far, gain, sems.at[3])
    got_weight = copy(weight_far, weight, sems.at[4])
    got_retention.wait()
    rows = jnp.concatenate([retention[...], jnp.zeros((8 - HEADS, TOK), F32)], axis=0)
    parts = pieces(rows)
    stacked = jnp.concatenate(
        [p[:, c * 128 : (c + 1) * 128] for c in range(TOK // 128) for p in parts], axis=0
    ).astype(BF16)
    first = lax.broadcasted_iota(jnp.int32, (128, 128), 0)
    second = lax.broadcasted_iota(jnp.int32, (128, 128), 1)
    upper = jnp.where(first <= second, 1.0, 0.0).astype(BF16)
    sums = mm(stacked, upper)
    offset = jnp.zeros((8, 1), F32)
    chunks = []
    for c in range(TOK // 128):
        own = sums[24 * c : 24 * c + 8] + sums[24 * c + 8 : 24 * c + 16] + sums[24 * c + 16 : 24 * c + 24]
        own = own + offset
        offset = own[:, 127:128]
        chunks.append(own)
    cum = jnp.concatenate(chunks, axis=1)
    cum_out[...] = cum
    tail = jnp.exp(offset - cum)
    decay = jnp.broadcast_to(jnp.exp(offset), (8, HEAD_DIM))
    got_keys.wait()
    got_values.wait()
    for h in range(HEADS):
        turned = keys[:, head(h)].T
        key_decayed = (turned.astype(F32) * tail[h : h + 1]).astype(BF16)
        out[h * PER_HEAD : (h + 1) * PER_HEAD] = message(
            mm(key_decayed, values[:, head(h)]), aux_tile(decay[h : h + 1])
        )
    got_gain.wait()
    got_weight.wait()


def decay_rows(aux):
    return jnp.broadcast_to(aux[0:1] + aux[1:2] + aux[2:3], (8, HEAD_DIM))


def forward_scan(arrived, out):
    state = jnp.zeros((8, HEAD_DIM), F32)
    for pair in range(BLOCKS // 2):
        both = []
        for b in (2 * pair, 2 * pair + 1):
            both.append(state)
            got = arrived[b].astype(F32)
            state = decay_rows(got[8:16]) * state + got[0:8]
        out[16 * pair : 16 * pair + 16] = jnp.concatenate(both, axis=0).astype(BF16)


def backward_scan_kernel(arrived, decays, out):
    state = jnp.zeros((8, HEAD_DIM), F32)
    for pair in reversed(range(BLOCKS // 2)):
        both = []
        for b in (2 * pair + 1, 2 * pair):
            both.append(state)
            state = decay_rows(decays[b].astype(F32)[8:16]) * state + arrived[b].astype(F32)[0:8]
        out[16 * pair : 16 * pair + 16] = jnp.concatenate(both[::-1], axis=0).astype(BF16)


def block_decay(logs, columns, h, i):
    rows, width = slice(i * HALF, (i + 1) * HALF), (i + 1) * HALF
    gap = columns[rows, h : h + 1] - logs[h : h + 1, 0:width]
    t = lax.broadcasted_iota(jnp.int32, (HALF, HALF), 0)
    s = lax.broadcasted_iota(jnp.int32, (HALF, HALF), 1)
    last = jnp.where(s <= t, gap[:, i * HALF :], FAR)
    return jnp.exp2(last if i == 0 else jnp.concatenate([gap[:, 0:HALF], last], axis=1))


def local_kernel(
    arrived, queries, keys, values, target, cum, states, local, turned, columns, target_square
):
    forward_scan(arrived, states)
    total = cum[:, TOK - 1 : TOK]
    start = jnp.exp(cum[...]) * SCALE
    tail = jnp.exp(total - cum[...])
    logs = cum[...] * LOG2E
    side = jnp.concatenate([logs + LOG2_SCALE, start, tail, jnp.zeros((104, TOK), F32)], axis=0).T
    columns[...] = side
    square = jnp.zeros((TOK, HEAD_DIM), F32)
    for h in range(HEADS):
        x = target[:, head(h)].astype(F32)
        square = square + x * x
        q, k, v = queries[:, head(h)], keys[:, head(h)], values[:, head(h)]
        turned[head(h), :] = (q.T.astype(F32) * start[h : h + 1]).astype(BF16)
        for i in range(2):
            rows, width = slice(i * HALF, (i + 1) * HALF), (i + 1) * HALF
            p = (mm(q[rows], k[0:width], NT) * block_decay(logs, side, h, i)).astype(BF16)
            local[rows, head(h)] = mm(p, v[0:width])
    target_square[...] = jnp.sum(square.T, axis=0, keepdims=True)


def output_kernel(queries, states, local, columns, target, gain, target_square, attn, sums):
    square = jnp.zeros((TOK, HEAD_DIM), F32)
    gain_square = square
    cross = square
    for h in range(HEADS):
        carried = mm(queries[:, head(h)], states[head(h), :])
        o = local[:, head(h)] + columns[:, 8 + h : 9 + h] * carried
        attn[:, head(h)] = o
        gained = gain[:, head(h)] * o
        square = square + o * o
        gain_square = gain_square + gained * gained
        cross = cross + gained * target[:, head(h)].astype(F32)
    four = jnp.concatenate(
        [jnp.sum(a.T, axis=0, keepdims=True) for a in (square, gain_square, cross)]
        + [target_square[...]],
        axis=0,
    )
    for d in range(8):
        sums[d] = four


def gradient_kernel(sums, attn, target, gain, weight, turned, out, grad_out):
    four = jnp.sum(sums[...], axis=0)
    mean_square = four[0:1] / HIDDEN_DIMENSION + EPS
    inverse = 1.0 / jnp.sqrt(mean_square)
    pred_square = four[1:2] / mean_square
    pred_cross = four[2:3] * inverse
    inner = weight[...] * (pred_square - pred_cross)
    a = weight[...] / mean_square
    b = weight[...] * inverse
    c = inner / (HIDDEN_DIMENSION * mean_square)
    side = jnp.concatenate([a, b, c, jnp.zeros((125, TOK), F32)], axis=0).T
    a, b, c = side[:, 0:1], side[:, 1:2], side[:, 2:3]
    gains, backs = [], []
    for h in range(HEADS):
        o, x, g = attn[:, head(h)], target[:, head(h)].astype(F32), gain[:, head(h)]
        error = a * (g * o) - b * x
        gains.append(jnp.sum(error * o, axis=0, keepdims=True))
        d = (error * g - c * o).astype(BF16)
        grad_out[:, head(h)] = d
        backs.append(mm(turned[head(h), :], d))
    gains = jnp.concatenate(gains, axis=0)
    high = gains.astype(BF16).astype(F32)
    tile = jnp.concatenate([high, gains - high], axis=0)
    for h in range(HEADS):
        out[h * PER_HEAD : (h + 1) * PER_HEAD] = message(backs[h], tile)


def local_gradient_kernel(
    grad_out, queries, keys_far, values_far, states, cum, columns, sums, arrived,
    grad_q, local_k, local_v, payoff, gain_out, keys, values, sems,
):
    got_keys = copy(keys_far, keys, sems.at[0])
    got_values = copy(values_far, values, sems.at[1])
    logs = cum[...] * LOG2E
    four = jnp.sum(sums[...], axis=0)
    mean_square = four[0:1] / HIDDEN_DIMENSION + EPS
    pred_square = four[1:2] / mean_square
    pred_cross = four[2:3] / jnp.sqrt(mean_square)
    payoff[...] = (pred_square - 2.0 * pred_cross + four[3:4]) / HIDDEN_DIMENSION
    gains = jnp.zeros((8, HEAD_DIM), F32)
    for b in range(BLOCKS):
        gains = gains + arrived[b].astype(F32)[8:16]
    gain_out[...] = (gains[0:HEADS] + gains[HEADS : 2 * HEADS]) / (BLOCKS * TOK)
    got_keys.wait()
    got_values.wait()
    for h in range(HEADS):
        q, k, v, d = queries[:, head(h)], keys[:, head(h)], values[:, head(h)], grad_out[:, head(h)]
        carried = columns[:, 8 + h : 9 + h] * mm(d, states[head(h), :], NT)
        parts, probs = [], []
        for i in range(2):
            rows, width = slice(i * HALF, (i + 1) * HALF), (i + 1) * HALF
            decay = block_decay(logs, columns, h, i)
            probs.append((mm(q[rows], k[0:width], NT) * decay).astype(BF16))
            gp = (mm(d[rows], v[0:width], NT) * decay).astype(BF16)
            parts.append(gp)
            grad_q[rows, head(h)] = (mm(gp, k[0:width]) + carried[rows]).astype(BF16)
        for side, near, far in ((local_k, parts, q), (local_v, probs, d)):
            early = jnp.concatenate([near[0], near[1][:, 0:HALF]], axis=0)
            side[0:HALF, head(h)] = mm(early, far, TN).astype(BF16)
            side[HALF:TOK, head(h)] = mm(near[1][:, HALF:TOK], far[HALF:TOK], TN).astype(BF16)


def final_kernel(
    states, keys, values, local_k, local_v, columns, grad_k_far, grad_v_far, grad_k, grad_v, sems
):
    moving = []
    for h in range(HEADS):
        tail, state = columns[:, 16 + h : 17 + h], states[head(h), :]
        for near, far, local, side, dims in (
            (grad_k, grad_k_far, local_k, values, NT),
            (grad_v, grad_v_far, local_v, keys, NN),
        ):
            moved = tail * mm(side[:, head(h)], state, dims)
            near[:, head(h)] = (local[:, head(h)].astype(F32) + moved).astype(BF16)
            moving.append(copy(near.at[:, head(h)], far.at[:, head(h)], sems.at[len(moving)]))
    for one in moving:
        one.wait()


NEAR = pl.BlockSpec(memory_space=pltpu.VMEM)
FAR_AWAY = pl.BlockSpec(memory_space=pltpu.HBM)


def call(kernel, outs, args, flops, name, far=(), far_outs=(), scratch=()):
    moved = sum(a.size * a.dtype.itemsize for a in args)
    moved += sum(o.size * o.dtype.itemsize for o in outs)
    placed = [pltpu.with_memory_space_constraint(a, pltpu.HBM) if i in far else a for i, a in enumerate(args)]
    return pl.pallas_call(
        kernel,
        out_shape=outs,
        in_specs=[FAR_AWAY if i in far else NEAR for i in range(len(args))],
        out_specs=[FAR_AWAY if i in far_outs else NEAR for i in range(len(outs))],
        scratch_shapes=scratch,
        compiler_params=pltpu.CompilerParams(vmem_limit_bytes=32 * 2**20),
        cost_estimate=pl.CostEstimate(flops=flops, bytes_accessed=moved, transcendentals=0),
        name=name,
    )(*placed)


def shape(dims, kind):
    return jax.ShapeDtypeStruct(dims, kind)


def exchange(x, axis):
    return lax.all_to_all(x, axis, 0, 0, tiled=True)


def local_part(queries, keys, values, retention, target, gain, weight):
    wide = TOK * TOK * HEAD_DIM * 2 * HEADS
    narrow = TOK * HEAD_DIM * HEAD_DIM * 2 * HEADS
    gain = gain.reshape(1, -1)
    weight = weight.reshape(1, -1)
    slices = shape((BLOCKS, 16, HEAD_DIM), BF16)
    full32 = shape((TOK, TOK), F32)
    full16 = shape((TOK, TOK), BF16)
    row = shape((1, TOK), F32)

    pair = [pltpu.VMEM((TOK, TOK), BF16)] * 2 + [pltpu.SemaphoreType.DMA((2,))]
    sent, cum, near_keys, near_values, gain, weight = call(
        summary_kernel,
        [slices, shape((8, TOK), F32), full16, full16, row, row],
        [retention, keys, values, gain, weight],
        narrow,
        "summary",
        far=(0, 1, 2, 3, 4),
        scratch=[pltpu.VMEM((HEADS, TOK), F32), pltpu.SemaphoreType.DMA((5,))],
    )
    arrived = exchange(sent, "ctx")
    back = shape((TOK, HEAD_DIM), BF16)
    states, local, turned, columns, target_square = call(
        local_kernel,
        [back, full32, full16, shape((TOK, 128), F32), row],
        [arrived, queries, near_keys, near_values, target, cum],
        2 * wide,
        "local",
    )
    states = exchange(states.reshape(BLOCKS, 8, HEAD_DIM), "ctx").reshape(TOK, HEAD_DIM)
    attn, sums = call(
        output_kernel,
        [full32, shape((8, 4, TOK), F32)],
        [queries, states, local, columns, target, gain, target_square],
        narrow,
        "output",
    )
    sums = exchange(sums, "head")
    sent, grad_out = call(
        gradient_kernel, [slices, full16], [sums, attn, target, gain, weight, turned], narrow, "gradient"
    )
    arrived_back = exchange(sent, "ctx")
    grad_q, local_k, local_v, payoff, gain_out = call(
        local_gradient_kernel,
        [full16, full16, full16, row, shape((HEADS, HEAD_DIM), F32)],
        [grad_out, queries, keys, values, states, cum, columns, sums, arrived_back],
        6 * wide,
        "local_gradient",
        far=(2, 3),
        scratch=pair,
    )
    [later] = call(backward_scan_kernel, [back], [arrived_back, arrived], 1000, "backward_scan")
    later = exchange(later.reshape(BLOCKS, 8, HEAD_DIM), "ctx").reshape(TOK, HEAD_DIM)
    grad_k, grad_v = call(
        final_kernel,
        [full16, full16],
        [later, keys, values, local_k, local_v, columns],
        2 * narrow,
        "final",
        far_outs=(0, 1),
        scratch=pair[:2] + [pltpu.SemaphoreType.DMA((2 * HEADS,))],
    )
    return payoff.reshape(-1), grad_q, grad_k, grad_v, gain_out.reshape(-1)


def solution(mesh):
    placed = (
        P("ctx", "head"),
        P("ctx", "head"),
        P("ctx", "head"),
        P("head", "ctx"),
        P("ctx", "head"),
        P("head"),
        P("ctx"),
    )
    return jax.shard_map(
        local_part,
        mesh=mesh,
        in_specs=placed,
        out_specs=(P("ctx"), P("ctx", "head"), P("ctx", "head"), P("ctx", "head"), P("head")),
        check_vma=False,
    )
```

```python
import math

import jax
import jax.numpy as jnp
from jax import lax
from jax.experimental import pallas as pl
from jax.experimental.pallas import tpu as pltpu
from jax.sharding import PartitionSpec as P

HEAD_DIM = 128
HIDDEN_DIMENSION = 4096
EPS = 1e-06
SCALE = HEAD_DIM ** (-0.5)
TOK = 512
HEADS = 4
BLOCKS = 64
PER_HEAD = BLOCKS // HEADS
HALF = TOK // 2
FAR = -1e9
LOG2E = math.log2(math.e)
LOG2_SCALE = math.log2(SCALE)

F32 = jnp.float32
BF16 = jnp.bfloat16

NN = (((1,), (0,)), ((), ()))
NT = (((1,), (1,)), ((), ()))
TN = (((0,), (0,)), ((), ()))


def mm(a, b, dims=NN):
    return lax.dot_general(a, b, dims, preferred_element_type=F32)


def head(h):
    return slice(h * HEAD_DIM, (h + 1) * HEAD_DIM)


def pieces(x):
    hi = x.astype(BF16).astype(F32)
    rest = x - hi
    mid = rest.astype(BF16).astype(F32)
    return hi, mid, rest - mid


def copy(source, target, sem):
    moving = pltpu.make_async_copy(source, target, sem)
    moving.start()
    return moving


def aux_tile(row):
    hi, mid, lo = pieces(row)
    at = lax.broadcasted_iota(jnp.int32, (4, HEAD_DIM), 0)
    return jnp.where(at == 0, hi, jnp.where(at == 1, mid, jnp.where(at == 2, lo, 0.0)))


def message(matrix, tile):
    data = matrix.reshape(PER_HEAD, 8, HEAD_DIM)
    aux = jnp.broadcast_to(tile[None], (PER_HEAD, 4, HEAD_DIM))
    return jnp.concatenate([data[:, 0:4], data[:, 4:8], aux], axis=2).astype(BF16)


def received(slices, b):
    got = slices[b].astype(F32)
    return jnp.concatenate([got[:, 0:128], got[:, 128:256]], axis=0), got[:, 256:384]


def summary_kernel(
    retention_far, keys_far, values_far, gain_far, weight_far,
    out, cum_out, keys, values, gain, weight, retention, sems,
):
    got_retention = copy(retention_far, retention, sems.at[0])
    got_keys = copy(keys_far, keys, sems.at[1])
    got_values = copy(values_far, values, sems.at[2])
    got_gain = copy(gain_far, gain, sems.at[3])
    got_weight = copy(weight_far, weight, sems.at[4])
    got_retention.wait()
    rows = jnp.concatenate([retention[...], jnp.zeros((8 - HEADS, TOK), F32)], axis=0)
    parts = pieces(rows)
    stacked = jnp.concatenate(
        [p[:, c * 128 : (c + 1) * 128] for c in range(TOK // 128) for p in parts], axis=0
    ).astype(BF16)
    first = lax.broadcasted_iota(jnp.int32, (128, 128), 0)
    second = lax.broadcasted_iota(jnp.int32, (128, 128), 1)
    upper = jnp.where(first <= second, 1.0, 0.0).astype(BF16)
    sums = mm(stacked, upper)
    offset = jnp.zeros((8, 1), F32)
    chunks = []
    for c in range(TOK // 128):
        own = sums[24 * c : 24 * c + 8] + sums[24 * c + 8 : 24 * c + 16] + sums[24 * c + 16 : 24 * c + 24]
        own = own + offset
        offset = own[:, 127:128]
        chunks.append(own)
    cum = jnp.concatenate(chunks, axis=1)
    cum_out[...] = cum
    tail = jnp.exp(offset - cum)
    decay = jnp.broadcast_to(jnp.exp(offset), (8, HEAD_DIM))
    got_keys.wait()
    decayed = []
    for h in range(HEADS):
        turned = keys[:, head(h)].T
        decayed.append((turned.astype(F32) * tail[h : h + 1]).astype(BF16))
    got_values.wait()
    for h in range(HEADS):
        out[h * PER_HEAD : (h + 1) * PER_HEAD] = message(
            mm(decayed[h], values[:, head(h)]), aux_tile(decay[h : h + 1])
        )
    got_gain.wait()
    got_weight.wait()


def decay_rows(aux):
    return jnp.broadcast_to(aux[0:1] + aux[1:2] + aux[2:3], (8, HEAD_DIM))


def forward_scan(arrived, out):
    state = jnp.zeros((8, HEAD_DIM), F32)
    for pair in range(BLOCKS // 2):
        both = []
        for b in (2 * pair, 2 * pair + 1):
            both.append(state)
            data, aux = received(arrived, b)
            state = decay_rows(aux) * state + data
        out[16 * pair : 16 * pair + 16] = jnp.concatenate(both, axis=0).astype(BF16)


def backward_scan_kernel(arrived, decays, out):
    state = jnp.zeros((8, HEAD_DIM), F32)
    for pair in reversed(range(BLOCKS // 2)):
        both = []
        for b in (2 * pair + 1, 2 * pair):
            both.append(state)
            state = decay_rows(received(decays, b)[1]) * state + received(arrived, b)[0]
        out[16 * pair : 16 * pair + 16] = jnp.concatenate(both[::-1], axis=0).astype(BF16)


def block_decay(logs, columns, h, i):
    rows, width = slice(i * HALF, (i + 1) * HALF), (i + 1) * HALF
    gap = columns[rows, h : h + 1] - logs[h : h + 1, 0:width]
    t = lax.broadcasted_iota(jnp.int32, (HALF, HALF), 0)
    s = lax.broadcasted_iota(jnp.int32, (HALF, HALF), 1)
    last = jnp.where(s <= t, gap[:, i * HALF :], FAR)
    return jnp.exp2(last if i == 0 else jnp.concatenate([gap[:, 0:HALF], last], axis=1))


def local_kernel(
    arrived, queries, keys, values, target, cum, states, local, turned, columns, target_square
):
    forward_scan(arrived, states)
    total = cum[:, TOK - 1 : TOK]
    start = jnp.exp(cum[...]) * SCALE
    tail = jnp.exp(total - cum[...])
    logs = cum[...] * LOG2E
    side = jnp.concatenate([logs + LOG2_SCALE, start, tail, jnp.zeros((104, TOK), F32)], axis=0).T
    columns[...] = side
    square = jnp.zeros((TOK, HEAD_DIM), F32)
    for h in range(HEADS):
        x = target[:, head(h)].astype(F32)
        square = square + x * x
        q, k, v = queries[:, head(h)], keys[:, head(h)], values[:, head(h)]
        turned[head(h), :] = (q.T.astype(F32) * start[h : h + 1]).astype(BF16)
        for i in range(2):
            rows, width = slice(i * HALF, (i + 1) * HALF), (i + 1) * HALF
            p = (mm(q[rows], k[0:width], NT) * block_decay(logs, side, h, i)).astype(BF16)
            local[rows, head(h)] = mm(p, v[0:width])
    target_square[...] = jnp.sum(square.T, axis=0, keepdims=True)


def output_kernel(queries, states, local, columns, target, gain, target_square, attn, sums):
    square = jnp.zeros((TOK, HEAD_DIM), F32)
    gain_square = square
    cross = square
    for h in range(HEADS):
        carried = mm(queries[:, head(h)], states[head(h), :])
        o = local[:, head(h)] + columns[:, 8 + h : 9 + h] * carried
        attn[:, head(h)] = o
        gained = gain[:, head(h)] * o
        square = square + o * o
        gain_square = gain_square + gained * gained
        cross = cross + gained * target[:, head(h)].astype(F32)
    four = jnp.concatenate(
        [jnp.sum(a.T, axis=0, keepdims=True) for a in (square, gain_square, cross)]
        + [target_square[...]],
        axis=0,
    )
    for d in range(8):
        sums[d] = four


def spread(*rows):
    parts = [p for row in rows for p in pieces(row)]
    parts.append(jnp.zeros((16 - len(parts), TOK), F32))
    width = len(rows) * HEAD_DIM
    part = lax.broadcasted_iota(jnp.int32, (16, width), 0)
    first = lax.broadcasted_iota(jnp.int32, (16, width), 1) // HEAD_DIM * 3
    chosen = jnp.where((part >= first) & (part < first + 3), 1.0, 0.0).astype(BF16)
    wide = mm(jnp.concatenate(parts, axis=0).astype(BF16), chosen, TN)
    return [wide[:, head(i)] for i in range(len(rows))]


def gradient_kernel(sums, attn, target, gain, weight, turned, out, grad_out):
    four = jnp.sum(sums[...], axis=0)
    mean_square = four[0:1] / HIDDEN_DIMENSION + EPS
    inverse = 1.0 / jnp.sqrt(mean_square)
    pred_square = four[1:2] / mean_square
    pred_cross = four[2:3] * inverse
    inner = weight[...] * (pred_square - pred_cross)
    a = weight[...] / mean_square
    b = weight[...] * inverse
    c = inner / (HIDDEN_DIMENSION * mean_square)
    a, b, c = spread(a, b, c)
    gains, backs = [], []
    for h in range(HEADS):
        o, x, g = attn[:, head(h)], target[:, head(h)].astype(F32), gain[:, head(h)]
        error = a * (g * o) - b * x
        gains.append(jnp.sum(error * o, axis=0, keepdims=True))
        d = (error * g - c * o).astype(BF16)
        grad_out[:, head(h)] = d
        backs.append(mm(turned[head(h), :], d))
    tile = jnp.concatenate(gains, axis=0)
    for h in range(HEADS):
        out[h * PER_HEAD : (h + 1) * PER_HEAD] = message(backs[h], tile)


def local_gradient_kernel(
    grad_out, queries, keys_far, values_far, states, cum, columns, sums, arrived,
    grad_q, local_k, local_v, payoff, gain_out, keys, values, sems,
):
    got_keys = copy(keys_far, keys, sems.at[0])
    got_values = copy(values_far, values, sems.at[1])
    logs = cum[...] * LOG2E
    four = jnp.sum(sums[...], axis=0)
    mean_square = four[0:1] / HIDDEN_DIMENSION + EPS
    pred_square = four[1:2] / mean_square
    pred_cross = four[2:3] / jnp.sqrt(mean_square)
    payoff[...] = (pred_square - 2.0 * pred_cross + four[3:4]) / HIDDEN_DIMENSION
    gains = jnp.zeros((HEADS, HEAD_DIM), F32)
    for b in range(BLOCKS):
        gains = gains + received(arrived, b)[1]
    gain_out[...] = gains / (BLOCKS * TOK)
    got_keys.wait()
    got_values.wait()
    for h in range(HEADS):
        q, k, v, d = queries[:, head(h)], keys[:, head(h)], values[:, head(h)], grad_out[:, head(h)]
        carried = columns[:, 8 + h : 9 + h] * mm(d, states[head(h), :], NT)
        parts, probs = [], []
        for i in range(2):
            rows, width = slice(i * HALF, (i + 1) * HALF), (i + 1) * HALF
            decay = block_decay(logs, columns, h, i)
            probs.append((mm(q[rows], k[0:width], NT) * decay).astype(BF16))
            gp = (mm(d[rows], v[0:width], NT) * decay).astype(BF16)
            parts.append(gp)
            grad_q[rows, head(h)] = (mm(gp, k[0:width]) + carried[rows]).astype(BF16)
        for side, near, far in ((local_k, parts, q), (local_v, probs, d)):
            early = jnp.concatenate([near[0], near[1][:, 0:HALF]], axis=0)
            side[0:HALF, head(h)] = mm(early, far, TN).astype(BF16)
            side[HALF:TOK, head(h)] = mm(near[1][:, HALF:TOK], far[HALF:TOK], TN).astype(BF16)


def final_kernel(
    states, keys, values, local_k, local_v, columns, grad_k_far, grad_v_far, grad_k, grad_v, sems
):
    moving = []
    for h in range(HEADS):
        tail, state = columns[:, 16 + h : 17 + h], states[head(h), :]
        for near, far, local, side, dims in (
            (grad_k, grad_k_far, local_k, values, NT),
            (grad_v, grad_v_far, local_v, keys, NN),
        ):
            moved = tail * mm(side[:, head(h)], state, dims)
            near[:, head(h)] = (local[:, head(h)].astype(F32) + moved).astype(BF16)
            moving.append(copy(near.at[:, head(h)], far.at[:, head(h)], sems.at[len(moving)]))
    for one in moving:
        one.wait()


NEAR = pl.BlockSpec(memory_space=pltpu.VMEM)
FAR_AWAY = pl.BlockSpec(memory_space=pltpu.HBM)


def call(kernel, outs, args, flops, name, far=(), far_outs=(), scratch=()):
    moved = sum(a.size * a.dtype.itemsize for a in args)
    moved += sum(o.size * o.dtype.itemsize for o in outs)
    placed = [pltpu.with_memory_space_constraint(a, pltpu.HBM) if i in far else a for i, a in enumerate(args)]
    return pl.pallas_call(
        kernel,
        out_shape=outs,
        in_specs=[FAR_AWAY if i in far else NEAR for i in range(len(args))],
        out_specs=[FAR_AWAY if i in far_outs else NEAR for i in range(len(outs))],
        scratch_shapes=scratch,
        compiler_params=pltpu.CompilerParams(vmem_limit_bytes=32 * 2**20),
        cost_estimate=pl.CostEstimate(flops=flops, bytes_accessed=moved, transcendentals=0),
        name=name,
    )(*placed)


def shape(dims, kind):
    return jax.ShapeDtypeStruct(dims, kind)


def exchange(x, axis):
    return lax.all_to_all(x, axis, 0, 0, tiled=True)


def local_part(queries, keys, values, retention, target, gain, weight):
    wide = TOK * TOK * HEAD_DIM * 2 * HEADS
    narrow = TOK * HEAD_DIM * HEAD_DIM * 2 * HEADS
    gain = gain.reshape(1, -1)
    weight = weight.reshape(1, -1)
    slices = shape((BLOCKS, 4, 3 * HEAD_DIM), BF16)
    full32 = shape((TOK, TOK), F32)
    full16 = shape((TOK, TOK), BF16)
    row = shape((1, TOK), F32)

    pair = [pltpu.VMEM((TOK, TOK), BF16)] * 2 + [pltpu.SemaphoreType.DMA((2,))]
    sent, cum, near_keys, near_values, gain, weight = call(
        summary_kernel,
        [slices, shape((8, TOK), F32), full16, full16, row, row],
        [retention, keys, values, gain, weight],
        narrow,
        "summary",
        far=(0, 1, 2, 3, 4),
        scratch=[pltpu.VMEM((HEADS, TOK), F32), pltpu.SemaphoreType.DMA((5,))],
    )
    arrived = exchange(sent, "ctx")
    back = shape((TOK, HEAD_DIM), BF16)
    states, local, turned, columns, target_square = call(
        local_kernel,
        [back, full32, full16, shape((TOK, 128), F32), row],
        [arrived, queries, near_keys, near_values, target, cum],
        2 * wide,
        "local",
    )
    states = exchange(states.reshape(BLOCKS, 8, HEAD_DIM), "ctx").reshape(TOK, HEAD_DIM)
    attn, sums = call(
        output_kernel,
        [full32, shape((8, 4, TOK), F32)],
        [queries, states, local, columns, target, gain, target_square],
        narrow,
        "output",
    )
    sums = exchange(sums, "head")
    sent, grad_out = call(
        gradient_kernel, [slices, full16], [sums, attn, target, gain, weight, turned], narrow, "gradient"
    )
    arrived_back = exchange(sent, "ctx")
    grad_q, local_k, local_v, payoff, gain_out = call(
        local_gradient_kernel,
        [full16, full16, full16, row, shape((HEADS, HEAD_DIM), F32)],
        [grad_out, queries, keys, values, states, cum, columns, sums, arrived_back],
        6 * wide,
        "local_gradient",
        far=(2, 3),
        scratch=pair,
    )
    [later] = call(backward_scan_kernel, [back], [arrived_back, arrived], 1000, "backward_scan")
    later = exchange(later.reshape(BLOCKS, 8, HEAD_DIM), "ctx").reshape(TOK, HEAD_DIM)
    grad_k, grad_v = call(
        final_kernel,
        [full16, full16],
        [later, keys, values, local_k, local_v, columns],
        2 * narrow,
        "final",
        far_outs=(0, 1),
        scratch=pair[:2] + [pltpu.SemaphoreType.DMA((2 * HEADS,))],
    )
    return payoff.reshape(-1), grad_q, grad_k, grad_v, gain_out.reshape(-1)


def solution(mesh):
    placed = (
        P("ctx", "head"),
        P("ctx", "head"),
        P("ctx", "head"),
        P("head", "ctx"),
        P("ctx", "head"),
        P("head"),
        P("ctx"),
    )
    return jax.shard_map(
        local_part,
        mesh=mesh,
        in_specs=placed,
        out_specs=(P("ctx"), P("ctx", "head"), P("ctx", "head"), P("ctx", "head"), P("head")),
        check_vma=False,
    )
```

```python
import math

import jax
import jax.numpy as jnp
from jax import lax
from jax.experimental import pallas as pl
from jax.experimental.pallas import tpu as pltpu
from jax.sharding import PartitionSpec as P

HEAD_DIM = 128
HIDDEN_DIMENSION = 4096
EPS = 1e-06
SCALE = HEAD_DIM ** (-0.5)
TOK = 512
HEADS = 4
BLOCKS = 64
PER_HEAD = BLOCKS // HEADS
HALF = TOK // 2
HALVES = EARLY, LATE = slice(0, HALF), slice(HALF, TOK)
TILES = (0, 0), (1, 0), (1, 1)
FAR = -1e9
LOG2E = math.log2(math.e)
LOG2_SCALE = math.log2(SCALE)

F32 = jnp.float32
BF16 = jnp.bfloat16

NN = (((1,), (0,)), ((), ()))
NT = (((1,), (1,)), ((), ()))
TN = (((0,), (0,)), ((), ()))


def mm(a, b, dims=NN):
    return lax.dot_general(a, b, dims, preferred_element_type=F32)


def head(h):
    return slice(h * HEAD_DIM, (h + 1) * HEAD_DIM)


def pieces(x):
    hi = x.astype(BF16).astype(F32)
    rest = x - hi
    mid = rest.astype(BF16).astype(F32)
    return hi, mid, rest - mid


def copy(source, target, sem):
    moving = pltpu.make_async_copy(source, target, sem)
    moving.start()
    return moving


def aux_tile(row):
    hi, mid, lo = pieces(row)
    at = lax.broadcasted_iota(jnp.int32, (4, HEAD_DIM), 0)
    return jnp.where(at == 0, hi, jnp.where(at == 1, mid, jnp.where(at == 2, lo, 0.0)))


def message(matrix, tile):
    data = matrix.reshape(PER_HEAD, 8, HEAD_DIM)
    aux = jnp.broadcast_to(tile[None], (PER_HEAD, 4, HEAD_DIM))
    return jnp.concatenate([data[:, 0:4], data[:, 4:8], aux], axis=2).astype(BF16)


def received(slices, b):
    got = slices[b].astype(F32)
    return jnp.concatenate([got[:, 0:128], got[:, 128:256]], axis=0), got[:, 256:384]


def summary_kernel(
    retention_far, keys_far, values_far, gain_far, weight_far,
    out, cum_out, keys, values, gain, weight, retention, sems,
):
    got_retention = copy(retention_far, retention, sems.at[0])
    got_keys = copy(keys_far, keys, sems.at[1])
    got_values = copy(values_far, values, sems.at[2])
    got_gain = copy(gain_far, gain, sems.at[3])
    got_weight = copy(weight_far, weight, sems.at[4])
    got_retention.wait()
    rows = jnp.concatenate([retention[...], jnp.zeros((8 - HEADS, TOK), F32)], axis=0)
    parts = pieces(rows)
    stacked = jnp.concatenate(
        [p[:, c * 128 : (c + 1) * 128] for c in range(TOK // 128) for p in parts], axis=0
    ).astype(BF16)
    first = lax.broadcasted_iota(jnp.int32, (128, 128), 0)
    second = lax.broadcasted_iota(jnp.int32, (128, 128), 1)
    upper = jnp.where(first <= second, 1.0, 0.0).astype(BF16)
    sums = mm(stacked, upper)
    offset = jnp.zeros((8, 1), F32)
    chunks = []
    for c in range(TOK // 128):
        own = sums[24 * c : 24 * c + 8] + sums[24 * c + 8 : 24 * c + 16] + sums[24 * c + 16 : 24 * c + 24]
        own = own + offset
        offset = own[:, 127:128]
        chunks.append(own)
    cum = jnp.concatenate(chunks, axis=1)
    cum_out[...] = cum
    tail = jnp.exp(offset - cum)
    decay = jnp.broadcast_to(jnp.exp(offset), (8, HEAD_DIM))
    got_keys.wait()
    decayed = []
    for h in range(HEADS):
        turned = keys[:, head(h)].T
        decayed.append((turned.astype(F32) * tail[h : h + 1]).astype(BF16))
    got_values.wait()
    for h in range(HEADS):
        out[h * PER_HEAD : (h + 1) * PER_HEAD] = message(
            mm(decayed[h], values[:, head(h)]), aux_tile(decay[h : h + 1])
        )
    got_gain.wait()
    got_weight.wait()


def decay_rows(aux):
    return jnp.broadcast_to(aux[0:1] + aux[1:2] + aux[2:3], (8, HEAD_DIM))


def forward_scan(arrived, out):
    state = jnp.zeros((8, HEAD_DIM), F32)
    for pair in range(BLOCKS // 2):
        both = []
        for b in (2 * pair, 2 * pair + 1):
            both.append(state)
            data, aux = received(arrived, b)
            state = decay_rows(aux) * state + data
        out[16 * pair : 16 * pair + 16] = jnp.concatenate(both, axis=0).astype(BF16)


def backward_scan_kernel(arrived, decays, out):
    state = jnp.zeros((8, HEAD_DIM), F32)
    for pair in reversed(range(BLOCKS // 2)):
        both = []
        for b in (2 * pair + 1, 2 * pair):
            both.append(state)
            state = decay_rows(received(decays, b)[1]) * state + received(arrived, b)[0]
        out[16 * pair : 16 * pair + 16] = jnp.concatenate(both[::-1], axis=0).astype(BF16)


def block_decay(logs, columns, h, i, j):
    gap = columns[HALVES[i], h : h + 1] - logs[h : h + 1, HALVES[j]]
    if i == j:
        t = lax.broadcasted_iota(jnp.int32, (HALF, HALF), 0)
        s = lax.broadcasted_iota(jnp.int32, (HALF, HALF), 1)
        gap = jnp.where(s <= t, gap, FAR)
    return jnp.exp2(gap)


def products(a, b):
    first = mm(a, b[EARLY], NT)
    return first[EARLY], first[LATE], mm(a[LATE], b[LATE], NT)


def along_rows(tiles, b):
    return mm(tiles[0], b[EARLY]), mm(jnp.concatenate(tiles[1:], axis=1), b)


def along_columns(tiles, b):
    return mm(jnp.concatenate(tiles[:2], axis=0), b, TN), mm(tiles[2], b[LATE], TN)


def local_kernel(
    arrived, queries, keys, values, target, cum, states, local, turned, columns, target_square
):
    forward_scan(arrived, states)
    total = cum[:, TOK - 1 : TOK]
    start = jnp.exp(cum[...]) * SCALE
    tail = jnp.exp(total - cum[...])
    logs = cum[...] * LOG2E
    side = jnp.concatenate([logs + LOG2_SCALE, start, tail, jnp.zeros((104, TOK), F32)], axis=0).T
    columns[...] = side
    probs = []
    for h in range(HEADS):
        scores = products(queries[:, head(h)], keys[:, head(h)])
        probs.append(
            [(a * block_decay(logs, side, h, *tile)).astype(BF16) for a, tile in zip(scores, TILES)]
        )
    for h in range(HEADS):
        for rows, part in zip(HALVES, along_rows(probs[h], values[:, head(h)])):
            local[rows, head(h)] = part
    square = jnp.zeros((TOK, HEAD_DIM), F32)
    for h in range(HEADS):
        x = target[:, head(h)].astype(F32)
        square = square + x * x
        turned[head(h), :] = (queries[:, head(h)].T.astype(F32) * start[h : h + 1]).astype(BF16)
    target_square[...] = jnp.sum(square.T, axis=0, keepdims=True)


def output_kernel(queries, states, local, columns, target, gain, target_square, attn, sums):
    square = jnp.zeros((TOK, HEAD_DIM), F32)
    gain_square = square
    cross = square
    carried = [mm(queries[:, head(h)], states[head(h), :]) for h in range(HEADS)]
    for h in range(HEADS):
        o = local[:, head(h)] + columns[:, 8 + h : 9 + h] * carried[h]
        attn[:, head(h)] = o
        gained = gain[:, head(h)] * o
        square = square + o * o
        gain_square = gain_square + gained * gained
        cross = cross + gained * target[:, head(h)].astype(F32)
    four = jnp.concatenate(
        [jnp.sum(a.T, axis=0, keepdims=True) for a in (square, gain_square, cross)]
        + [target_square[...]],
        axis=0,
    )
    for d in range(8):
        sums[d] = four


def spread(*rows):
    parts = [p for row in rows for p in pieces(row)]
    parts.append(jnp.zeros((16 - len(parts), TOK), F32))
    width = len(rows) * HEAD_DIM
    part = lax.broadcasted_iota(jnp.int32, (16, width), 0)
    first = lax.broadcasted_iota(jnp.int32, (16, width), 1) // HEAD_DIM * 3
    chosen = jnp.where((part >= first) & (part < first + 3), 1.0, 0.0).astype(BF16)
    wide = mm(jnp.concatenate(parts, axis=0).astype(BF16), chosen, TN)
    return [wide[:, head(i)] for i in range(len(rows))]


def gradient_kernel(sums, attn, target, gain, weight, turned, out, grad_out):
    four = jnp.sum(sums[...], axis=0)
    mean_square = four[0:1] / HIDDEN_DIMENSION + EPS
    inverse = 1.0 / jnp.sqrt(mean_square)
    pred_square = four[1:2] / mean_square
    pred_cross = four[2:3] * inverse
    inner = weight[...] * (pred_square - pred_cross)
    a = weight[...] / mean_square
    b = weight[...] * inverse
    c = inner / (HIDDEN_DIMENSION * mean_square)
    a, b, c = spread(a, b, c)
    gains, backs = [], []
    for h in range(HEADS):
        o, x, g = attn[:, head(h)], target[:, head(h)].astype(F32), gain[:, head(h)]
        error = a * (g * o) - b * x
        gains.append(jnp.sum(error * o, axis=0, keepdims=True))
        d = (error * g - c * o).astype(BF16)
        grad_out[:, head(h)] = d
        backs.append(mm(turned[head(h), :], d))
    tile = jnp.concatenate(gains, axis=0)
    for h in range(HEADS):
        out[h * PER_HEAD : (h + 1) * PER_HEAD] = message(backs[h], tile)


def local_gradient_kernel(
    grad_out, queries, keys_far, values_far, states, cum, columns, sums, arrived,
    grad_q, local_k, local_v, payoff, gain_out, keys, values, sems,
):
    got_keys = copy(keys_far, keys, sems.at[0])
    got_values = copy(values_far, values, sems.at[1])
    logs = cum[...] * LOG2E
    four = jnp.sum(sums[...], axis=0)
    mean_square = four[0:1] / HIDDEN_DIMENSION + EPS
    pred_square = four[1:2] / mean_square
    pred_cross = four[2:3] / jnp.sqrt(mean_square)
    payoff[...] = (pred_square - 2.0 * pred_cross + four[3:4]) / HIDDEN_DIMENSION
    gains = jnp.zeros((HEADS, HEAD_DIM), F32)
    for b in range(BLOCKS):
        gains = gains + received(arrived, b)[1]
    gain_out[...] = gains / (BLOCKS * TOK)
    got_keys.wait()
    got_values.wait()
    for h in range(HEADS):
        q, k, v, d = queries[:, head(h)], keys[:, head(h)], values[:, head(h)], grad_out[:, head(h)]
        carried = columns[:, 8 + h : 9 + h] * mm(d, states[head(h), :], NT)
        decays = [block_decay(logs, columns, h, *tile) for tile in TILES]
        probs = [(a * decay).astype(BF16) for a, decay in zip(products(q, k), decays)]
        grads = [(a * decay).astype(BF16) for a, decay in zip(products(d, v), decays)]
        for rows, part in zip(HALVES, along_rows(grads, k)):
            grad_q[rows, head(h)] = (part + carried[rows]).astype(BF16)
        for side, tiles, far in ((local_k, grads, q), (local_v, probs, d)):
            for rows, part in zip(HALVES, along_columns(tiles, far)):
                side[rows, head(h)] = part.astype(BF16)


def final_kernel(
    states, keys, values, local_k, local_v, columns, grad_k_far, grad_v_far, grad_k, grad_v, sems
):
    moving = []
    for h in range(HEADS):
        tail, state = columns[:, 16 + h : 17 + h], states[head(h), :]
        for near, far, local, side, dims in (
            (grad_k, grad_k_far, local_k, values, NT),
            (grad_v, grad_v_far, local_v, keys, NN),
        ):
            moved = tail * mm(side[:, head(h)], state, dims)
            near[:, head(h)] = (local[:, head(h)].astype(F32) + moved).astype(BF16)
            moving.append(copy(near.at[:, head(h)], far.at[:, head(h)], sems.at[len(moving)]))
    for one in moving:
        one.wait()


NEAR = pl.BlockSpec(memory_space=pltpu.VMEM)
FAR_AWAY = pl.BlockSpec(memory_space=pltpu.HBM)


def call(kernel, outs, args, flops, name, far=(), far_outs=(), scratch=()):
    moved = sum(a.size * a.dtype.itemsize for a in args)
    moved += sum(o.size * o.dtype.itemsize for o in outs)
    placed = [pltpu.with_memory_space_constraint(a, pltpu.HBM) if i in far else a for i, a in enumerate(args)]
    return pl.pallas_call(
        kernel,
        out_shape=outs,
        in_specs=[FAR_AWAY if i in far else NEAR for i in range(len(args))],
        out_specs=[FAR_AWAY if i in far_outs else NEAR for i in range(len(outs))],
        scratch_shapes=scratch,
        compiler_params=pltpu.CompilerParams(vmem_limit_bytes=32 * 2**20),
        cost_estimate=pl.CostEstimate(flops=flops, bytes_accessed=moved, transcendentals=0),
        name=name,
    )(*placed)


def shape(dims, kind):
    return jax.ShapeDtypeStruct(dims, kind)


def exchange(x, axis):
    return lax.all_to_all(x, axis, 0, 0, tiled=True)


def local_part(queries, keys, values, retention, target, gain, weight):
    wide = TOK * TOK * HEAD_DIM * 2 * HEADS
    narrow = TOK * HEAD_DIM * HEAD_DIM * 2 * HEADS
    gain = gain.reshape(1, -1)
    weight = weight.reshape(1, -1)
    slices = shape((BLOCKS, 4, 3 * HEAD_DIM), BF16)
    full32 = shape((TOK, TOK), F32)
    full16 = shape((TOK, TOK), BF16)
    row = shape((1, TOK), F32)

    pair = [pltpu.VMEM((TOK, TOK), BF16)] * 2 + [pltpu.SemaphoreType.DMA((2,))]
    sent, cum, near_keys, near_values, gain, weight = call(
        summary_kernel,
        [slices, shape((8, TOK), F32), full16, full16, row, row],
        [retention, keys, values, gain, weight],
        narrow,
        "summary",
        far=(0, 1, 2, 3, 4),
        scratch=[pltpu.VMEM((HEADS, TOK), F32), pltpu.SemaphoreType.DMA((5,))],
    )
    arrived = exchange(sent, "ctx")
    back = shape((TOK, HEAD_DIM), BF16)
    states, local, turned, columns, target_square = call(
        local_kernel,
        [back, full32, full16, shape((TOK, 128), F32), row],
        [arrived, queries, near_keys, near_values, target, cum],
        2 * wide,
        "local",
    )
    states = exchange(states.reshape(BLOCKS, 8, HEAD_DIM), "ctx").reshape(TOK, HEAD_DIM)
    attn, sums = call(
        output_kernel,
        [full32, shape((8, 4, TOK), F32)],
        [queries, states, local, columns, target, gain, target_square],
        narrow,
        "output",
    )
    sums = exchange(sums, "head")
    sent, grad_out = call(
        gradient_kernel, [slices, full16], [sums, attn, target, gain, weight, turned], narrow, "gradient"
    )
    arrived_back = exchange(sent, "ctx")
    grad_q, local_k, local_v, payoff, gain_out = call(
        local_gradient_kernel,
        [full16, full16, full16, row, shape((HEADS, HEAD_DIM), F32)],
        [grad_out, queries, keys, values, states, cum, columns, sums, arrived_back],
        6 * wide,
        "local_gradient",
        far=(2, 3),
        scratch=pair,
    )
    [later] = call(backward_scan_kernel, [back], [arrived_back, arrived], 1000, "backward_scan")
    later = exchange(later.reshape(BLOCKS, 8, HEAD_DIM), "ctx").reshape(TOK, HEAD_DIM)
    grad_k, grad_v = call(
        final_kernel,
        [full16, full16],
        [later, keys, values, local_k, local_v, columns],
        2 * narrow,
        "final",
        far_outs=(0, 1),
        scratch=pair[:2] + [pltpu.SemaphoreType.DMA((2 * HEADS,))],
    )
    return payoff.reshape(-1), grad_q, grad_k, grad_v, gain_out.reshape(-1)


def solution(mesh):
    placed = (
        P("ctx", "head"),
        P("ctx", "head"),
        P("ctx", "head"),
        P("head", "ctx"),
        P("ctx", "head"),
        P("head"),
        P("ctx"),
    )
    return jax.shard_map(
        local_part,
        mesh=mesh,
        in_specs=placed,
        out_specs=(P("ctx"), P("ctx", "head"), P("ctx", "head"), P("ctx", "head"), P("head")),
        check_vma=False,
    )
```

```python
import math

import jax
import jax.numpy as jnp
from jax import lax
from jax.experimental import pallas as pl
from jax.experimental.pallas import tpu as pltpu
from jax.sharding import PartitionSpec as P

HEAD_DIM = 128
HIDDEN_DIMENSION = 4096
EPS = 1e-06
SCALE = HEAD_DIM ** (-0.5)
TOK = 512
HEADS = 4
BLOCKS = 64
PER_HEAD = BLOCKS // HEADS
FIRST = {"ctx": 36, "head": 4}
HALF = TOK // 2
HALVES = EARLY, LATE = slice(0, HALF), slice(HALF, TOK)
TILES = (0, 0), (1, 0), (1, 1)
FAR = -1e9
LOG2E = math.log2(math.e)
LOG2_SCALE = math.log2(SCALE)

F32 = jnp.float32
BF16 = jnp.bfloat16

NN = (((1,), (0,)), ((), ()))
NT = (((1,), (1,)), ((), ()))
TN = (((0,), (0,)), ((), ()))


def mm(a, b, dims=NN):
    return lax.dot_general(a, b, dims, preferred_element_type=F32)


def head(h):
    return slice(h * HEAD_DIM, (h + 1) * HEAD_DIM)


def pieces(x):
    hi = x.astype(BF16).astype(F32)
    rest = x - hi
    mid = rest.astype(BF16).astype(F32)
    return hi, mid, rest - mid


def copy(source, target, sem):
    moving = pltpu.make_async_copy(source, target, sem)
    moving.start()
    return moving


def aux_tile(row):
    hi, mid, lo = pieces(row)
    at = lax.broadcasted_iota(jnp.int32, (4, HEAD_DIM), 0)
    return jnp.where(at == 0, hi, jnp.where(at == 1, mid, jnp.where(at == 2, lo, 0.0)))


def message(matrix, tile):
    data = matrix.reshape(PER_HEAD, 8, HEAD_DIM)
    aux = jnp.broadcast_to(tile[None], (PER_HEAD, 4, HEAD_DIM))
    return jnp.concatenate([data[:, 0:4], data[:, 4:8], aux], axis=2).astype(BF16)


def slot(b):
    return (b - FIRST["ctx"]) % BLOCKS


def received(slices, b):
    got = slices[slot(b)].astype(F32)
    return jnp.concatenate([got[:, 0:128], got[:, 128:256]], axis=0), got[:, 256:384]


def summary_kernel(
    retention_far, keys_far, values_far, gain_far, weight_far,
    out, cum_out, keys, values, gain, weight, retention, sems,
):
    got_retention = copy(retention_far, retention, sems.at[0])
    got_keys = copy(keys_far, keys, sems.at[1])
    got_values = copy(values_far, values, sems.at[2])
    got_gain = copy(gain_far, gain, sems.at[3])
    got_weight = copy(weight_far, weight, sems.at[4])
    got_retention.wait()
    rows = jnp.concatenate([retention[...], jnp.zeros((8 - HEADS, TOK), F32)], axis=0)
    parts = pieces(rows)
    stacked = jnp.concatenate(
        [p[:, c * 128 : (c + 1) * 128] for c in range(TOK // 128) for p in parts], axis=0
    ).astype(BF16)
    first = lax.broadcasted_iota(jnp.int32, (128, 128), 0)
    second = lax.broadcasted_iota(jnp.int32, (128, 128), 1)
    upper = jnp.where(first <= second, 1.0, 0.0).astype(BF16)
    sums = mm(stacked, upper)
    offset = jnp.zeros((8, 1), F32)
    chunks = []
    for c in range(TOK // 128):
        own = sums[24 * c : 24 * c + 8] + sums[24 * c + 8 : 24 * c + 16] + sums[24 * c + 16 : 24 * c + 24]
        own = own + offset
        offset = own[:, 127:128]
        chunks.append(own)
    cum = jnp.concatenate(chunks, axis=1)
    cum_out[...] = cum
    tail = jnp.exp(offset - cum)
    decay = jnp.broadcast_to(jnp.exp(offset), (8, HEAD_DIM))
    got_keys.wait()
    decayed = []
    for h in range(HEADS):
        turned = keys[:, head(h)].T
        decayed.append((turned.astype(F32) * tail[h : h + 1]).astype(BF16))
    got_values.wait()
    for h in range(HEADS):
        out[h * PER_HEAD : (h + 1) * PER_HEAD] = message(
            mm(decayed[h], values[:, head(h)]), aux_tile(decay[h : h + 1])
        )
    got_gain.wait()
    got_weight.wait()


def decay_rows(aux):
    return jnp.broadcast_to(aux[0:1] + aux[1:2] + aux[2:3], (8, HEAD_DIM))


def forward_scan(arrived, out):
    state = jnp.zeros((8, HEAD_DIM), F32)
    for pair in range(BLOCKS // 2):
        both = []
        for b in (2 * pair, 2 * pair + 1):
            both.append(state)
            data, aux = received(arrived, b)
            state = decay_rows(aux) * state + data
        at = 8 * slot(2 * pair)
        out[at : at + 16] = jnp.concatenate(both, axis=0).astype(BF16)


def backward_scan_kernel(arrived, decays, out):
    state = jnp.zeros((8, HEAD_DIM), F32)
    for pair in reversed(range(BLOCKS // 2)):
        both = []
        for b in (2 * pair + 1, 2 * pair):
            both.append(state)
            state = decay_rows(received(decays, b)[1]) * state + received(arrived, b)[0]
        at = 8 * slot(2 * pair)
        out[at : at + 16] = jnp.concatenate(both[::-1], axis=0).astype(BF16)


def block_decay(logs, columns, h, i, j):
    gap = columns[HALVES[i], h : h + 1] - logs[h : h + 1, HALVES[j]]
    if i == j:
        t = lax.broadcasted_iota(jnp.int32, (HALF, HALF), 0)
        s = lax.broadcasted_iota(jnp.int32, (HALF, HALF), 1)
        gap = jnp.where(s <= t, gap, FAR)
    return jnp.exp2(gap)


def products(a, b):
    first = mm(a, b[EARLY], NT)
    return first[EARLY], first[LATE], mm(a[LATE], b[LATE], NT)


def along_rows(tiles, b):
    return mm(tiles[0], b[EARLY]), mm(jnp.concatenate(tiles[1:], axis=1), b)


def along_columns(tiles, b):
    return mm(jnp.concatenate(tiles[:2], axis=0), b, TN), mm(tiles[2], b[LATE], TN)


def local_kernel(
    arrived, queries, keys, values, target, cum, states, local, turned, columns, target_square
):
    forward_scan(arrived, states)
    total = cum[:, TOK - 1 : TOK]
    start = jnp.exp(cum[...]) * SCALE
    tail = jnp.exp(total - cum[...])
    logs = cum[...] * LOG2E
    side = jnp.concatenate([logs + LOG2_SCALE, start, tail, jnp.zeros((104, TOK), F32)], axis=0).T
    columns[...] = side
    probs = []
    for h in range(HEADS):
        scores = products(queries[:, head(h)], keys[:, head(h)])
        probs.append(
            [(a * block_decay(logs, side, h, *tile)).astype(BF16) for a, tile in zip(scores, TILES)]
        )
    for h in range(HEADS):
        for rows, part in zip(HALVES, along_rows(probs[h], values[:, head(h)])):
            local[rows, head(h)] = part
    square = jnp.zeros((TOK, HEAD_DIM), F32)
    for h in range(HEADS):
        x = target[:, head(h)].astype(F32)
        square = square + x * x
        turned[head(h), :] = (queries[:, head(h)].T.astype(F32) * start[h : h + 1]).astype(BF16)
    target_square[...] = jnp.sum(square.T, axis=0, keepdims=True)


def output_kernel(queries, states, local, columns, target, gain, target_square, attn, sums):
    square = jnp.zeros((TOK, HEAD_DIM), F32)
    gain_square = square
    cross = square
    carried = [mm(queries[:, head(h)], states[head(h), :]) for h in range(HEADS)]
    for h in range(HEADS):
        o = local[:, head(h)] + columns[:, 8 + h : 9 + h] * carried[h]
        attn[:, head(h)] = o
        gained = gain[:, head(h)] * o
        square = square + o * o
        gain_square = gain_square + gained * gained
        cross = cross + gained * target[:, head(h)].astype(F32)
    four = jnp.concatenate(
        [jnp.sum(a.T, axis=0, keepdims=True) for a in (square, gain_square, cross)]
        + [target_square[...]],
        axis=0,
    )
    for d in range(8):
        sums[d] = four


def spread(*rows):
    parts = [p for row in rows for p in pieces(row)]
    parts.append(jnp.zeros((16 - len(parts), TOK), F32))
    width = len(rows) * HEAD_DIM
    part = lax.broadcasted_iota(jnp.int32, (16, width), 0)
    first = lax.broadcasted_iota(jnp.int32, (16, width), 1) // HEAD_DIM * 3
    chosen = jnp.where((part >= first) & (part < first + 3), 1.0, 0.0).astype(BF16)
    wide = mm(jnp.concatenate(parts, axis=0).astype(BF16), chosen, TN)
    return [wide[:, head(i)] for i in range(len(rows))]


def gradient_kernel(sums, attn, target, gain, weight, turned, out, grad_out):
    four = jnp.sum(sums[...], axis=0)
    mean_square = four[0:1] / HIDDEN_DIMENSION + EPS
    inverse = 1.0 / jnp.sqrt(mean_square)
    pred_square = four[1:2] / mean_square
    pred_cross = four[2:3] * inverse
    inner = weight[...] * (pred_square - pred_cross)
    a = weight[...] / mean_square
    b = weight[...] * inverse
    c = inner / (HIDDEN_DIMENSION * mean_square)
    a, b, c = spread(a, b, c)
    gains, backs = [], []
    for h in range(HEADS):
        o, x, g = attn[:, head(h)], target[:, head(h)].astype(F32), gain[:, head(h)]
        error = a * (g * o) - b * x
        gains.append(jnp.sum(error * o, axis=0, keepdims=True))
        d = (error * g - c * o).astype(BF16)
        grad_out[:, head(h)] = d
        backs.append(mm(turned[head(h), :], d))
    tile = jnp.concatenate(gains, axis=0)
    for h in range(HEADS):
        out[h * PER_HEAD : (h + 1) * PER_HEAD] = message(backs[h], tile)


def local_gradient_kernel(
    grad_out, queries, keys_far, values_far, states, cum, columns, sums, arrived,
    grad_q, local_k, local_v, payoff, gain_out, keys, values, sems,
):
    got_keys = copy(keys_far, keys, sems.at[0])
    got_values = copy(values_far, values, sems.at[1])
    logs = cum[...] * LOG2E
    four = jnp.sum(sums[...], axis=0)
    mean_square = four[0:1] / HIDDEN_DIMENSION + EPS
    pred_square = four[1:2] / mean_square
    pred_cross = four[2:3] / jnp.sqrt(mean_square)
    payoff[...] = (pred_square - 2.0 * pred_cross + four[3:4]) / HIDDEN_DIMENSION
    gains = jnp.zeros((HEADS, HEAD_DIM), F32)
    for b in range(BLOCKS):
        gains = gains + received(arrived, b)[1]
    gain_out[...] = gains / (BLOCKS * TOK)
    got_keys.wait()
    got_values.wait()
    for h in range(HEADS):
        q, k, v, d = queries[:, head(h)], keys[:, head(h)], values[:, head(h)], grad_out[:, head(h)]
        carried = columns[:, 8 + h : 9 + h] * mm(d, states[head(h), :], NT)
        decays = [block_decay(logs, columns, h, *tile) for tile in TILES]
        probs = [(a * decay).astype(BF16) for a, decay in zip(products(q, k), decays)]
        grads = [(a * decay).astype(BF16) for a, decay in zip(products(d, v), decays)]
        for rows, part in zip(HALVES, along_rows(grads, k)):
            grad_q[rows, head(h)] = (part + carried[rows]).astype(BF16)
        for side, tiles, far in ((local_k, grads, q), (local_v, probs, d)):
            for rows, part in zip(HALVES, along_columns(tiles, far)):
                side[rows, head(h)] = part.astype(BF16)


def final_kernel(
    states, keys, values, local_k, local_v, columns, grad_k_far, grad_v_far, grad_k, grad_v, sems
):
    moving = []
    for h in range(HEADS):
        tail, state = columns[:, 16 + h : 17 + h], states[head(h), :]
        for near, far, local, side, dims in (
            (grad_k, grad_k_far, local_k, values, NT),
            (grad_v, grad_v_far, local_v, keys, NN),
        ):
            moved = tail * mm(side[:, head(h)], state, dims)
            near[:, head(h)] = (local[:, head(h)].astype(F32) + moved).astype(BF16)
            moving.append(copy(near.at[:, head(h)], far.at[:, head(h)], sems.at[len(moving)]))
    for one in moving:
        one.wait()


NEAR = pl.BlockSpec(memory_space=pltpu.VMEM)
FAR_AWAY = pl.BlockSpec(memory_space=pltpu.HBM)


def call(kernel, outs, args, flops, name, far=(), far_outs=(), scratch=()):
    moved = sum(a.size * a.dtype.itemsize for a in args)
    moved += sum(o.size * o.dtype.itemsize for o in outs)
    placed = [pltpu.with_memory_space_constraint(a, pltpu.HBM) if i in far else a for i, a in enumerate(args)]
    return pl.pallas_call(
        kernel,
        out_shape=outs,
        in_specs=[FAR_AWAY if i in far else NEAR for i in range(len(args))],
        out_specs=[FAR_AWAY if i in far_outs else NEAR for i in range(len(outs))],
        scratch_shapes=scratch,
        compiler_params=pltpu.CompilerParams(vmem_limit_bytes=32 * 2**20),
        cost_estimate=pl.CostEstimate(flops=flops, bytes_accessed=moved, transcendentals=0),
        name=name,
    )(*placed)


def shape(dims, kind):
    return jax.ShapeDtypeStruct(dims, kind)


def exchange(x, axis):
    count, first = x.shape[0], FIRST[axis]
    order = [(first + i) % count for i in range(count)]
    return lax.all_to_all(x, axis, 0, 0, tiled=True, axis_index_groups=[order])


def local_part(queries, keys, values, retention, target, gain, weight):
    wide = TOK * TOK * HEAD_DIM * 2 * HEADS
    narrow = TOK * HEAD_DIM * HEAD_DIM * 2 * HEADS
    gain = gain.reshape(1, -1)
    weight = weight.reshape(1, -1)
    slices = shape((BLOCKS, 4, 3 * HEAD_DIM), BF16)
    full32 = shape((TOK, TOK), F32)
    full16 = shape((TOK, TOK), BF16)
    row = shape((1, TOK), F32)

    pair = [pltpu.VMEM((TOK, TOK), BF16)] * 2 + [pltpu.SemaphoreType.DMA((2,))]
    sent, cum, near_keys, near_values, gain, weight = call(
        summary_kernel,
        [slices, shape((8, TOK), F32), full16, full16, row, row],
        [retention, keys, values, gain, weight],
        narrow,
        "summary",
        far=(0, 1, 2, 3, 4),
        scratch=[pltpu.VMEM((HEADS, TOK), F32), pltpu.SemaphoreType.DMA((5,))],
    )
    arrived = exchange(sent, "ctx")
    back = shape((TOK, HEAD_DIM), BF16)
    states, local, turned, columns, target_square = call(
        local_kernel,
        [back, full32, full16, shape((TOK, 128), F32), row],
        [arrived, queries, near_keys, near_values, target, cum],
        2 * wide,
        "local",
    )
    states = exchange(states.reshape(BLOCKS, 8, HEAD_DIM), "ctx").reshape(TOK, HEAD_DIM)
    attn, sums = call(
        output_kernel,
        [full32, shape((8, 4, TOK), F32)],
        [queries, states, local, columns, target, gain, target_square],
        narrow,
        "output",
    )
    sums = exchange(sums, "head")
    sent, grad_out = call(
        gradient_kernel, [slices, full16], [sums, attn, target, gain, weight, turned], narrow, "gradient"
    )
    arrived_back = exchange(sent, "ctx")
    grad_q, local_k, local_v, payoff, gain_out = call(
        local_gradient_kernel,
        [full16, full16, full16, row, shape((HEADS, HEAD_DIM), F32)],
        [grad_out, queries, keys, values, states, cum, columns, sums, arrived_back],
        6 * wide,
        "local_gradient",
        far=(2, 3),
        scratch=pair,
    )
    [later] = call(backward_scan_kernel, [back], [arrived_back, arrived], 1000, "backward_scan")
    later = exchange(later.reshape(BLOCKS, 8, HEAD_DIM), "ctx").reshape(TOK, HEAD_DIM)
    grad_k, grad_v = call(
        final_kernel,
        [full16, full16],
        [later, keys, values, local_k, local_v, columns],
        2 * narrow,
        "final",
        far_outs=(0, 1),
        scratch=pair[:2] + [pltpu.SemaphoreType.DMA((2 * HEADS,))],
    )
    return payoff.reshape(-1), grad_q, grad_k, grad_v, gain_out.reshape(-1)


def solution(mesh):
    placed = (
        P("ctx", "head"),
        P("ctx", "head"),
        P("ctx", "head"),
        P("head", "ctx"),
        P("ctx", "head"),
        P("head"),
        P("ctx"),
    )
    return jax.shard_map(
        local_part,
        mesh=mesh,
        in_specs=placed,
        out_specs=(P("ctx"), P("ctx", "head"), P("ctx", "head"), P("ctx", "head"), P("head")),
        check_vma=False,
    )
```

```python
import math

import jax
import jax.numpy as jnp
from jax import lax
from jax.experimental import pallas as pl
from jax.experimental.pallas import tpu as pltpu
from jax.sharding import PartitionSpec as P

HEAD_DIM = 128
HIDDEN_DIMENSION = 4096
EPS = 1e-06
SCALE = HEAD_DIM ** (-0.5)
TOK = 512
HEADS = 4
BLOCKS = 64
PER_HEAD = BLOCKS // HEADS
FIRST = {"ctx": 36, "head": 4}
HALF = TOK // 2
HALVES = EARLY, LATE = slice(0, HALF), slice(HALF, TOK)
TILES = (0, 0), (1, 0), (1, 1)
FAR = -1e9
LOG2E = math.log2(math.e)
LOG2_SCALE = math.log2(SCALE)

F32 = jnp.float32
BF16 = jnp.bfloat16

NN = (((1,), (0,)), ((), ()))
NT = (((1,), (1,)), ((), ()))
TN = (((0,), (0,)), ((), ()))


def mm(a, b, dims=NN):
    return lax.dot_general(a, b, dims, preferred_element_type=F32)


def head(h):
    return slice(h * HEAD_DIM, (h + 1) * HEAD_DIM)


def pieces(x):
    hi = x.astype(BF16).astype(F32)
    rest = x - hi
    mid = rest.astype(BF16).astype(F32)
    return hi, mid, rest - mid


def copy(source, target, sem):
    moving = pltpu.make_async_copy(source, target, sem)
    moving.start()
    return moving


def aux_tile(row):
    hi, mid, lo = pieces(row)
    at = lax.broadcasted_iota(jnp.int32, (4, HEAD_DIM), 0)
    return jnp.where(at == 0, hi, jnp.where(at == 1, mid, jnp.where(at == 2, lo, 0.0)))


def message(matrix, tile):
    data = matrix.reshape(PER_HEAD, 8, HEAD_DIM)
    aux = jnp.broadcast_to(tile[None], (PER_HEAD, 4, HEAD_DIM))
    return jnp.concatenate([data[:, 0:4], data[:, 4:8], aux], axis=2).astype(BF16)


def slot(b):
    return (b - FIRST["ctx"]) % BLOCKS


def received(slices, b):
    got = slices[slot(b)].astype(F32)
    return jnp.concatenate([got[:, 0:128], got[:, 128:256]], axis=0), got[:, 256:384]


def summary_kernel(
    retention_far, keys_far, values_far, gain_far, weight_far,
    out, cum_out, keys, values, gain, weight, retention, sems,
):
    got_retention = copy(retention_far, retention, sems.at[0])
    got_keys = copy(keys_far, keys, sems.at[1])
    got_values = copy(values_far, values, sems.at[2])
    got_gain = copy(gain_far, gain, sems.at[3])
    got_weight = copy(weight_far, weight, sems.at[4])
    got_retention.wait()
    rows = jnp.concatenate([retention[...], jnp.zeros((8 - HEADS, TOK), F32)], axis=0)
    parts = pieces(rows)
    stacked = jnp.concatenate(
        [p[:, c * 128 : (c + 1) * 128] for c in range(TOK // 128) for p in parts], axis=0
    ).astype(BF16)
    first = lax.broadcasted_iota(jnp.int32, (128, 128), 0)
    second = lax.broadcasted_iota(jnp.int32, (128, 128), 1)
    upper = jnp.where(first <= second, 1.0, 0.0).astype(BF16)
    sums = mm(stacked, upper)
    offset = jnp.zeros((8, 1), F32)
    chunks = []
    for c in range(TOK // 128):
        own = sums[24 * c : 24 * c + 8] + sums[24 * c + 8 : 24 * c + 16] + sums[24 * c + 16 : 24 * c + 24]
        own = own + offset
        offset = own[:, 127:128]
        chunks.append(own)
    cum = jnp.concatenate(chunks, axis=1)
    cum_out[...] = cum
    tail = jnp.exp(offset - cum)
    decay = jnp.broadcast_to(jnp.exp(offset), (8, HEAD_DIM))
    got_keys.wait()
    decayed = []
    for h in range(HEADS):
        turned = keys[:, head(h)].T
        decayed.append((turned.astype(F32) * tail[h : h + 1]).astype(BF16))
    got_values.wait()
    for h in range(HEADS):
        out[h * PER_HEAD : (h + 1) * PER_HEAD] = message(
            mm(decayed[h], values[:, head(h)]), aux_tile(decay[h : h + 1])
        )
    got_gain.wait()
    got_weight.wait()


def decay_rows(aux):
    return jnp.broadcast_to(aux[0:1] + aux[1:2] + aux[2:3], (8, HEAD_DIM))


def forward_scan(arrived, out):
    state = jnp.zeros((8, HEAD_DIM), F32)
    for pair in range(BLOCKS // 2):
        both = []
        for b in (2 * pair, 2 * pair + 1):
            both.append(state)
            data, aux = received(arrived, b)
            state = decay_rows(aux) * state + data
        at = 8 * slot(2 * pair)
        out[at : at + 16] = jnp.concatenate(both, axis=0).astype(BF16)


def backward_scan_kernel(arrived, decays, mark, out):
    state = jnp.zeros((8, HEAD_DIM), F32)
    for pair in reversed(range(BLOCKS // 2)):
        both = []
        for b in (2 * pair + 1, 2 * pair):
            both.append(state)
            state = decay_rows(received(decays, b)[1]) * state + received(arrived, b)[0]
        at = 8 * slot(2 * pair)
        out[at : at + 16] = jnp.concatenate(both[::-1], axis=0).astype(BF16)


def block_decay(logs, columns, h, i, j):
    gap = columns[HALVES[i], h : h + 1] - logs[h : h + 1, HALVES[j]]
    if i == j:
        t = lax.broadcasted_iota(jnp.int32, (HALF, HALF), 0)
        s = lax.broadcasted_iota(jnp.int32, (HALF, HALF), 1)
        gap = jnp.where(s <= t, gap, FAR)
    return jnp.exp2(gap)


def products(a, b):
    first = mm(a, b[EARLY], NT)
    return first[EARLY], first[LATE], mm(a[LATE], b[LATE], NT)


def along_rows(tiles, b):
    return mm(tiles[0], b[EARLY]), mm(jnp.concatenate(tiles[1:], axis=1), b)


def along_columns(tiles, b):
    return mm(jnp.concatenate(tiles[:2], axis=0), b, TN), mm(tiles[2], b[LATE], TN)


def local_kernel(
    arrived, queries, keys, values, target, cum, states, local, turned, columns, target_square
):
    forward_scan(arrived, states)
    total = cum[:, TOK - 1 : TOK]
    start = jnp.exp(cum[...]) * SCALE
    tail = jnp.exp(total - cum[...])
    logs = cum[...] * LOG2E
    side = jnp.concatenate([logs + LOG2_SCALE, start, tail, jnp.zeros((104, TOK), F32)], axis=0).T
    columns[...] = side
    probs = []
    for h in range(HEADS):
        scores = products(queries[:, head(h)], keys[:, head(h)])
        probs.append(
            [(a * block_decay(logs, side, h, *tile)).astype(BF16) for a, tile in zip(scores, TILES)]
        )
    for h in range(HEADS):
        for rows, part in zip(HALVES, along_rows(probs[h], values[:, head(h)])):
            local[rows, head(h)] = part
    square = jnp.zeros((TOK, HEAD_DIM), F32)
    for h in range(HEADS):
        x = target[:, head(h)].astype(F32)
        square = square + x * x
        turned[head(h), :] = (queries[:, head(h)].T.astype(F32) * start[h : h + 1]).astype(BF16)
    target_square[...] = jnp.sum(square.T, axis=0, keepdims=True)


def output_kernel(queries, states, local, columns, target, gain, target_square, attn, sums):
    square = jnp.zeros((TOK, HEAD_DIM), F32)
    gain_square = square
    cross = square
    carried = [mm(queries[:, head(h)], states[head(h), :]) for h in range(HEADS)]
    for h in range(HEADS):
        o = local[:, head(h)] + columns[:, 8 + h : 9 + h] * carried[h]
        attn[:, head(h)] = o
        gained = gain[:, head(h)] * o
        square = square + o * o
        gain_square = gain_square + gained * gained
        cross = cross + gained * target[:, head(h)].astype(F32)
    four = jnp.concatenate(
        [jnp.sum(a.T, axis=0, keepdims=True) for a in (square, gain_square, cross)]
        + [target_square[...]],
        axis=0,
    )
    for d in range(8):
        sums[d] = four


def spread(*rows):
    parts = [p for row in rows for p in pieces(row)]
    parts.append(jnp.zeros((16 - len(parts), TOK), F32))
    width = len(rows) * HEAD_DIM
    part = lax.broadcasted_iota(jnp.int32, (16, width), 0)
    first = lax.broadcasted_iota(jnp.int32, (16, width), 1) // HEAD_DIM * 3
    chosen = jnp.where((part >= first) & (part < first + 3), 1.0, 0.0).astype(BF16)
    wide = mm(jnp.concatenate(parts, axis=0).astype(BF16), chosen, TN)
    return [wide[:, head(i)] for i in range(len(rows))]


def gradient_kernel(
    sums, attn, target, gain, weight, turned, out_far, grad_out, out, sems
):
    four = jnp.sum(sums[...], axis=0)
    mean_square = four[0:1] / HIDDEN_DIMENSION + EPS
    inverse = 1.0 / jnp.sqrt(mean_square)
    pred_square = four[1:2] / mean_square
    pred_cross = four[2:3] * inverse
    inner = weight[...] * (pred_square - pred_cross)
    a = weight[...] / mean_square
    b = weight[...] * inverse
    c = inner / (HIDDEN_DIMENSION * mean_square)
    a, b, c = spread(a, b, c)
    gains, backs = [], []
    for h in range(HEADS):
        o, x, g = attn[:, head(h)], target[:, head(h)].astype(F32), gain[:, head(h)]
        error = a * (g * o) - b * x
        gains.append(jnp.sum(error * o, axis=0, keepdims=True))
        d = (error * g - c * o).astype(BF16)
        grad_out[:, head(h)] = d
        backs.append(mm(turned[head(h), :], d))
    tile = jnp.concatenate(gains, axis=0)
    moving = []
    for h in range(HEADS):
        owners = slice(h * PER_HEAD, (h + 1) * PER_HEAD)
        out[owners] = message(backs[h], tile)
        moving.append(copy(out.at[owners], out_far.at[owners], sems.at[h]))
    for one in moving:
        one.wait()


def local_gradient_kernel(
    grad_out, queries, keys_far, values_far, states, cum, columns, sums,
    grad_q, local_k, local_v, payoff, mark, keys, values, sems,
):
    got_keys = copy(keys_far, keys, sems.at[0])
    got_values = copy(values_far, values, sems.at[1])
    logs = cum[...] * LOG2E
    four = jnp.sum(sums[...], axis=0)
    mean_square = four[0:1] / HIDDEN_DIMENSION + EPS
    pred_square = four[1:2] / mean_square
    pred_cross = four[2:3] / jnp.sqrt(mean_square)
    payoff[...] = (pred_square - 2.0 * pred_cross + four[3:4]) / HIDDEN_DIMENSION
    mark[...] = jnp.zeros((8, HEAD_DIM), F32)
    got_keys.wait()
    got_values.wait()
    for h in range(HEADS):
        q, k, v, d = queries[:, head(h)], keys[:, head(h)], values[:, head(h)], grad_out[:, head(h)]
        carried = columns[:, 8 + h : 9 + h] * mm(d, states[head(h), :], NT)
        decays = [block_decay(logs, columns, h, *tile) for tile in TILES]
        probs = [(a * decay).astype(BF16) for a, decay in zip(products(q, k), decays)]
        grads = [(a * decay).astype(BF16) for a, decay in zip(products(d, v), decays)]
        for rows, part in zip(HALVES, along_rows(grads, k)):
            grad_q[rows, head(h)] = (part + carried[rows]).astype(BF16)
        for side, tiles, far in ((local_k, grads, q), (local_v, probs, d)):
            for rows, part in zip(HALVES, along_columns(tiles, far)):
                side[rows, head(h)] = part.astype(BF16)


def final_kernel(
    states, keys, values, local_k, local_v, columns, arrived,
    grad_k_far, grad_v_far, gain_far, grad_k, grad_v, gain, sems,
):
    gains = jnp.zeros((HEADS, HEAD_DIM), F32)
    for b in range(BLOCKS):
        gains = gains + received(arrived, b)[1]
    gain[...] = gains / (BLOCKS * TOK)
    moving = [copy(gain, gain_far, sems.at[0])]
    for h in range(HEADS):
        tail, state = columns[:, 16 + h : 17 + h], states[head(h), :]
        for near, far, local, side, dims in (
            (grad_k, grad_k_far, local_k, values, NT),
            (grad_v, grad_v_far, local_v, keys, NN),
        ):
            moved = tail * mm(side[:, head(h)], state, dims)
            near[:, head(h)] = (local[:, head(h)].astype(F32) + moved).astype(BF16)
            moving.append(copy(near.at[:, head(h)], far.at[:, head(h)], sems.at[len(moving)]))
    for one in moving:
        one.wait()


NEAR = pl.BlockSpec(memory_space=pltpu.VMEM)
FAR_AWAY = pl.BlockSpec(memory_space=pltpu.HBM)


def call(kernel, outs, args, flops, name, far=(), far_outs=(), scratch=()):
    moved = sum(a.size * a.dtype.itemsize for a in args)
    moved += sum(o.size * o.dtype.itemsize for o in outs)
    placed = [pltpu.with_memory_space_constraint(a, pltpu.HBM) if i in far else a for i, a in enumerate(args)]
    return pl.pallas_call(
        kernel,
        out_shape=outs,
        in_specs=[FAR_AWAY if i in far else NEAR for i in range(len(args))],
        out_specs=[FAR_AWAY if i in far_outs else NEAR for i in range(len(outs))],
        scratch_shapes=scratch,
        compiler_params=pltpu.CompilerParams(vmem_limit_bytes=32 * 2**20),
        cost_estimate=pl.CostEstimate(flops=flops, bytes_accessed=moved, transcendentals=0),
        name=name,
    )(*placed)


def shape(dims, kind):
    return jax.ShapeDtypeStruct(dims, kind)


def exchange(x, axis):
    count, first = x.shape[0], FIRST[axis]
    order = [(first + i) % count for i in range(count)]
    return lax.all_to_all(x, axis, 0, 0, tiled=True, axis_index_groups=[order])


def local_part(queries, keys, values, retention, target, gain, weight):
    wide = TOK * TOK * HEAD_DIM * 2 * HEADS
    narrow = TOK * HEAD_DIM * HEAD_DIM * 2 * HEADS
    gain = gain.reshape(1, -1)
    weight = weight.reshape(1, -1)
    slices = shape((BLOCKS, 4, 3 * HEAD_DIM), BF16)
    full32 = shape((TOK, TOK), F32)
    full16 = shape((TOK, TOK), BF16)
    row = shape((1, TOK), F32)

    pair = [pltpu.VMEM((TOK, TOK), BF16)] * 2 + [pltpu.SemaphoreType.DMA((2,))]
    sent, cum, near_keys, near_values, gain, weight = call(
        summary_kernel,
        [slices, shape((8, TOK), F32), full16, full16, row, row],
        [retention, keys, values, gain, weight],
        narrow,
        "summary",
        far=(0, 1, 2, 3, 4),
        scratch=[pltpu.VMEM((HEADS, TOK), F32), pltpu.SemaphoreType.DMA((5,))],
    )
    arrived = exchange(sent, "ctx")
    back = shape((TOK, HEAD_DIM), BF16)
    states, local, turned, columns, target_square = call(
        local_kernel,
        [back, full32, full16, shape((TOK, 128), F32), row],
        [arrived, queries, near_keys, near_values, target, cum],
        2 * wide,
        "local",
    )
    states = exchange(states.reshape(BLOCKS, 8, HEAD_DIM), "ctx").reshape(TOK, HEAD_DIM)
    attn, sums = call(
        output_kernel,
        [full32, shape((8, 4, TOK), F32)],
        [queries, states, local, columns, target, gain, target_square],
        narrow,
        "output",
    )
    sums = exchange(sums, "head")
    sent, grad_out = call(
        gradient_kernel,
        [slices, full16],
        [sums, attn, target, gain, weight, turned],
        narrow,
        "gradient",
        far_outs=(0,),
        scratch=[pltpu.VMEM(slices.shape, BF16), pltpu.SemaphoreType.DMA((HEADS,))],
    )
    arrived_back = exchange(sent, "ctx")
    grad_q, local_k, local_v, payoff, mark = call(
        local_gradient_kernel,
        [full16, full16, full16, row, shape((8, HEAD_DIM), F32)],
        [grad_out, queries, keys, values, states, cum, columns, sums],
        6 * wide,
        "local_gradient",
        far=(2, 3),
        scratch=pair,
    )
    [later] = call(backward_scan_kernel, [back], [arrived_back, arrived, mark], 1000, "backward_scan")
    later = exchange(later.reshape(BLOCKS, 8, HEAD_DIM), "ctx").reshape(TOK, HEAD_DIM)
    grad_k, grad_v, gain_out = call(
        final_kernel,
        [full16, full16, shape((HEADS, HEAD_DIM), F32)],
        [later, keys, values, local_k, local_v, columns, arrived_back],
        2 * narrow,
        "final",
        far_outs=(0, 1, 2),
        scratch=pair[:2]
        + [pltpu.VMEM((HEADS, HEAD_DIM), F32), pltpu.SemaphoreType.DMA((2 * HEADS + 1,))],
    )
    return payoff.reshape(-1), grad_q, grad_k, grad_v, gain_out.reshape(-1)


def solution(mesh):
    placed = (
        P("ctx", "head"),
        P("ctx", "head"),
        P("ctx", "head"),
        P("head", "ctx"),
        P("ctx", "head"),
        P("head"),
        P("ctx"),
    )
    return jax.shard_map(
        local_part,
        mesh=mesh,
        in_specs=placed,
        out_specs=(P("ctx"), P("ctx", "head"), P("ctx", "head"), P("ctx", "head"), P("head")),
        check_vma=False,
    )
```

```python
import math

import jax
import jax.numpy as jnp
from jax import lax
from jax.experimental import pallas as pl
from jax.experimental.pallas import tpu as pltpu
from jax.sharding import PartitionSpec as P

HEAD_DIM = 128
HIDDEN_DIMENSION = 4096
EPS = 1e-06
SCALE = HEAD_DIM ** (-0.5)
TOK = 512
HEADS = 4
BLOCKS = 64
PER_HEAD = BLOCKS // HEADS
FIRST = {"ctx": 36, "head": 4}
HALF = TOK // 2
HALVES = EARLY, LATE = slice(0, HALF), slice(HALF, TOK)
TILES = (0, 0), (1, 0), (1, 1)
FAR = -1e9
LOG2E = math.log2(math.e)
LOG2_SCALE = math.log2(SCALE)

F32 = jnp.float32
BF16 = jnp.bfloat16

NN = (((1,), (0,)), ((), ()))
NT = (((1,), (1,)), ((), ()))
TN = (((0,), (0,)), ((), ()))


def mm(a, b, dims=NN):
    return lax.dot_general(a, b, dims, preferred_element_type=F32)


def head(h):
    return slice(h * HEAD_DIM, (h + 1) * HEAD_DIM)


def pieces(x):
    hi = x.astype(BF16).astype(F32)
    rest = x - hi
    mid = rest.astype(BF16).astype(F32)
    return hi, mid, rest - mid


def copy(source, target, sem):
    moving = pltpu.make_async_copy(source, target, sem)
    moving.start()
    return moving


def aux_tile(row):
    hi, mid, lo = pieces(row)
    at = lax.broadcasted_iota(jnp.int32, (4, HEAD_DIM), 0)
    return jnp.where(at == 0, hi, jnp.where(at == 1, mid, jnp.where(at == 2, lo, 0.0)))


def message(matrix, tile):
    data = matrix.reshape(PER_HEAD, 8, HEAD_DIM)
    aux = jnp.broadcast_to(tile[None], (PER_HEAD, 4, HEAD_DIM))
    return jnp.concatenate([data[:, 0:4], data[:, 4:8], aux], axis=2).astype(BF16)


def slot(b):
    return (b - FIRST["ctx"]) % BLOCKS


def received(slices, b):
    got = slices[slot(b)].astype(F32)
    return jnp.concatenate([got[:, 0:128], got[:, 128:256]], axis=0), got[:, 256:384]


def summary_kernel(
    retention_far, keys_far, values_far, gain_far, weight_far,
    out, cum_out, keys, values, gain, weight, retention, sems,
):
    got_retention = copy(retention_far, retention, sems.at[0])
    got_keys = copy(keys_far, keys, sems.at[1])
    got_values = copy(values_far, values, sems.at[2])
    got_gain = copy(gain_far, gain, sems.at[3])
    got_weight = copy(weight_far, weight, sems.at[4])
    got_retention.wait()
    rows = jnp.concatenate([retention[...], jnp.zeros((8 - HEADS, TOK), F32)], axis=0)
    parts = pieces(rows)
    stacked = jnp.concatenate(
        [p[:, c * 128 : (c + 1) * 128] for c in range(TOK // 128) for p in parts], axis=0
    ).astype(BF16)
    first = lax.broadcasted_iota(jnp.int32, (128, 128), 0)
    second = lax.broadcasted_iota(jnp.int32, (128, 128), 1)
    upper = jnp.where(first <= second, 1.0, 0.0).astype(BF16)
    sums = mm(stacked, upper)
    offset = jnp.zeros((8, 1), F32)
    chunks = []
    for c in range(TOK // 128):
        own = sums[24 * c : 24 * c + 8] + sums[24 * c + 8 : 24 * c + 16] + sums[24 * c + 16 : 24 * c + 24]
        own = own + offset
        offset = own[:, 127:128]
        chunks.append(own)
    cum = jnp.concatenate(chunks, axis=1)
    cum_out[...] = cum
    tail = jnp.exp(offset - cum)
    decay = jnp.broadcast_to(jnp.exp(offset), (8, HEAD_DIM))
    got_keys.wait()
    decayed = []
    for h in range(HEADS):
        turned = keys[:, head(h)].T
        decayed.append((turned.astype(F32) * tail[h : h + 1]).astype(BF16))
    got_values.wait()
    for h in range(HEADS):
        out[h * PER_HEAD : (h + 1) * PER_HEAD] = message(
            mm(decayed[h], values[:, head(h)]), aux_tile(decay[h : h + 1])
        )
    got_gain.wait()
    got_weight.wait()


def decay_rows(aux):
    return jnp.broadcast_to(aux[0:1] + aux[1:2] + aux[2:3], (8, HEAD_DIM))


def forward_scan(arrived, out):
    state = jnp.zeros((8, HEAD_DIM), F32)
    for pair in range(BLOCKS // 2):
        both = []
        for b in (2 * pair, 2 * pair + 1):
            both.append(state)
            data, aux = received(arrived, b)
            state = decay_rows(aux) * state + data
        at = 8 * slot(2 * pair)
        out[at : at + 16] = jnp.concatenate(both, axis=0).astype(BF16)


def backward_scan_kernel(arrived, decays, mark, out):
    state = jnp.zeros((8, HEAD_DIM), F32)
    for pair in reversed(range(BLOCKS // 2)):
        both = []
        for b in (2 * pair + 1, 2 * pair):
            both.append(state)
            state = decay_rows(received(decays, b)[1]) * state + received(arrived, b)[0]
        at = 8 * slot(2 * pair)
        out[at : at + 16] = jnp.concatenate(both[::-1], axis=0).astype(BF16)


def block_decay(logs, columns, h, i, j):
    gap = columns[HALVES[i], h : h + 1] - logs[h : h + 1, HALVES[j]]
    if i == j:
        t = lax.broadcasted_iota(jnp.int32, (HALF, HALF), 0)
        s = lax.broadcasted_iota(jnp.int32, (HALF, HALF), 1)
        gap = jnp.where(s <= t, gap, FAR)
    return jnp.exp2(gap)


def products(a, b):
    first = mm(a, b[EARLY], NT)
    return first[EARLY], first[LATE], mm(a[LATE], b[LATE], NT)


def along_rows(tiles, b):
    return mm(tiles[0], b[EARLY]), mm(jnp.concatenate(tiles[1:], axis=1), b)


def along_columns(tiles, b):
    return mm(jnp.concatenate(tiles[:2], axis=0), b, TN), mm(tiles[2], b[LATE], TN)


def local_kernel(
    arrived, queries, keys, values, target, cum, states, local, turned, columns, target_square
):
    forward_scan(arrived, states)
    total = cum[:, TOK - 1 : TOK]
    start = jnp.exp(cum[...]) * SCALE
    tail = jnp.exp(total - cum[...])
    logs = cum[...] * LOG2E
    side = jnp.concatenate([logs + LOG2_SCALE, start, tail, jnp.zeros((104, TOK), F32)], axis=0).T
    columns[...] = side
    probs = []
    for h in range(HEADS):
        scores = products(queries[:, head(h)], keys[:, head(h)])
        probs.append(
            [(a * block_decay(logs, side, h, *tile)).astype(BF16) for a, tile in zip(scores, TILES)]
        )
    for h in range(HEADS):
        for rows, part in zip(HALVES, along_rows(probs[h], values[:, head(h)])):
            local[rows, head(h)] = part
    square = jnp.zeros((TOK, HEAD_DIM), F32)
    for h in range(HEADS):
        x = target[:, head(h)].astype(F32)
        square = square + x * x
        turned[head(h), :] = (queries[:, head(h)].T.astype(F32) * start[h : h + 1]).astype(BF16)
    target_square[...] = jnp.sum(square.T, axis=0, keepdims=True)


def output_kernel(queries, states, local, columns, target, gain, target_square, attn, sums):
    square = jnp.zeros((TOK, HEAD_DIM), F32)
    gain_square = square
    cross = square
    carried = [mm(queries[:, head(h)], states[head(h), :]) for h in range(HEADS)]
    for h in range(HEADS):
        o = local[:, head(h)] + columns[:, 8 + h : 9 + h] * carried[h]
        attn[:, head(h)] = o
        gained = gain[:, head(h)] * o
        square = square + o * o
        gain_square = gain_square + gained * gained
        cross = cross + gained * target[:, head(h)].astype(F32)
    four = jnp.concatenate(
        [jnp.sum(a.T, axis=0, keepdims=True) for a in (square, gain_square, cross)]
        + [target_square[...]],
        axis=0,
    )
    for d in range(8):
        sums[d] = four


def spread(*rows):
    parts = [p for row in rows for p in pieces(row)]
    parts.append(jnp.zeros((16 - len(parts), TOK), F32))
    width = len(rows) * HEAD_DIM
    part = lax.broadcasted_iota(jnp.int32, (16, width), 0)
    first = lax.broadcasted_iota(jnp.int32, (16, width), 1) // HEAD_DIM * 3
    chosen = jnp.where((part >= first) & (part < first + 3), 1.0, 0.0).astype(BF16)
    wide = mm(jnp.concatenate(parts, axis=0).astype(BF16), chosen, TN)
    return [wide[:, head(i)] for i in range(len(rows))]


def gradient_kernel(
    sums, attn, target, gain, weight, turned, out_far, grad_out, out, sems
):
    four = jnp.sum(sums[...], axis=0)
    mean_square = four[0:1] / HIDDEN_DIMENSION + EPS
    inverse = 1.0 / jnp.sqrt(mean_square)
    pred_square = four[1:2] / mean_square
    pred_cross = four[2:3] * inverse
    inner = weight[...] * (pred_square - pred_cross)
    a = weight[...] / mean_square
    b = weight[...] * inverse
    c = inner / (HIDDEN_DIMENSION * mean_square)
    a, b, c = spread(a, b, c)
    gains, backs = [], []
    for h in range(HEADS):
        o, x, g = attn[:, head(h)], target[:, head(h)].astype(F32), gain[:, head(h)]
        error = a * (g * o) - b * x
        gains.append(jnp.sum(error * o, axis=0, keepdims=True))
        d = (error * g - c * o).astype(BF16)
        grad_out[:, head(h)] = d
        backs.append(mm(turned[head(h), :], d))
    tile = jnp.concatenate(gains, axis=0)
    moving = []
    for h in range(HEADS):
        owners = slice(h * PER_HEAD, (h + 1) * PER_HEAD)
        out[owners] = message(backs[h], tile)
        moving.append(copy(out.at[owners], out_far.at[owners], sems.at[h]))
    for one in moving:
        one.wait()


def local_gradient_kernel(
    grad_out, queries, keys, values_far, states, cum, columns, sums,
    grad_q, local_k, local_v, payoff, mark, values, sem,
):
    got_values = copy(values_far, values, sem)
    logs = cum[...] * LOG2E
    four = jnp.sum(sums[...], axis=0)
    mean_square = four[0:1] / HIDDEN_DIMENSION + EPS
    pred_square = four[1:2] / mean_square
    pred_cross = four[2:3] / jnp.sqrt(mean_square)
    payoff[...] = (pred_square - 2.0 * pred_cross + four[3:4]) / HIDDEN_DIMENSION
    mark[...] = jnp.zeros((8, HEAD_DIM), F32)
    decays, probs = [], []
    for h in range(HEADS):
        decays.append([block_decay(logs, columns, h, *tile) for tile in TILES])
        scores = products(queries[:, head(h)], keys[:, head(h)])
        probs.append([(a * decay).astype(BF16) for a, decay in zip(scores, decays[h])])
    got_values.wait()
    for h in range(HEADS):
        q, k, v, d = queries[:, head(h)], keys[:, head(h)], values[:, head(h)], grad_out[:, head(h)]
        carried = columns[:, 8 + h : 9 + h] * mm(d, states[head(h), :], NT)
        grads = [(a * decay).astype(BF16) for a, decay in zip(products(d, v), decays[h])]
        for rows, part in zip(HALVES, along_rows(grads, k)):
            grad_q[rows, head(h)] = (part + carried[rows]).astype(BF16)
        for side, tiles, far in ((local_k, grads, q), (local_v, probs[h], d)):
            for rows, part in zip(HALVES, along_columns(tiles, far)):
                side[rows, head(h)] = part.astype(BF16)


def final_kernel(
    states, keys, values, local_k, local_v, columns, arrived,
    grad_k_far, grad_v_far, gain_far, grad_k, grad_v, gain, sems,
):
    gains = jnp.zeros((HEADS, HEAD_DIM), F32)
    for b in range(BLOCKS):
        gains = gains + received(arrived, b)[1]
    gain[...] = gains / (BLOCKS * TOK)
    moving = [copy(gain, gain_far, sems.at[0])]
    for h in range(HEADS):
        tail, state = columns[:, 16 + h : 17 + h], states[head(h), :]
        for near, far, local, side, dims in (
            (grad_k, grad_k_far, local_k, values, NT),
            (grad_v, grad_v_far, local_v, keys, NN),
        ):
            moved = tail * mm(side[:, head(h)], state, dims)
            near[:, head(h)] = (local[:, head(h)].astype(F32) + moved).astype(BF16)
            moving.append(copy(near.at[:, head(h)], far.at[:, head(h)], sems.at[len(moving)]))
    for one in moving:
        one.wait()


NEAR = pl.BlockSpec(memory_space=pltpu.VMEM)
FAR_AWAY = pl.BlockSpec(memory_space=pltpu.HBM)


def call(kernel, outs, args, flops, name, far=(), far_outs=(), scratch=()):
    moved = sum(a.size * a.dtype.itemsize for a in args)
    moved += sum(o.size * o.dtype.itemsize for o in outs)
    placed = [pltpu.with_memory_space_constraint(a, pltpu.HBM) if i in far else a for i, a in enumerate(args)]
    return pl.pallas_call(
        kernel,
        out_shape=outs,
        in_specs=[FAR_AWAY if i in far else NEAR for i in range(len(args))],
        out_specs=[FAR_AWAY if i in far_outs else NEAR for i in range(len(outs))],
        scratch_shapes=scratch,
        compiler_params=pltpu.CompilerParams(vmem_limit_bytes=32 * 2**20),
        cost_estimate=pl.CostEstimate(flops=flops, bytes_accessed=moved, transcendentals=0),
        name=name,
    )(*placed)


def shape(dims, kind):
    return jax.ShapeDtypeStruct(dims, kind)


def exchange(x, axis):
    count, first = x.shape[0], FIRST[axis]
    order = [(first + i) % count for i in range(count)]
    return lax.all_to_all(x, axis, 0, 0, tiled=True, axis_index_groups=[order])


def local_part(queries, keys, values, retention, target, gain, weight):
    wide = TOK * TOK * HEAD_DIM * 2 * HEADS
    narrow = TOK * HEAD_DIM * HEAD_DIM * 2 * HEADS
    gain = gain.reshape(1, -1)
    weight = weight.reshape(1, -1)
    slices = shape((BLOCKS, 4, 3 * HEAD_DIM), BF16)
    full32 = shape((TOK, TOK), F32)
    full16 = shape((TOK, TOK), BF16)
    row = shape((1, TOK), F32)

    pair = [pltpu.VMEM((TOK, TOK), BF16)] * 2 + [pltpu.SemaphoreType.DMA((2,))]
    sent, cum, near_keys, near_values, gain, weight = call(
        summary_kernel,
        [slices, shape((8, TOK), F32), full16, full16, row, row],
        [retention, keys, values, gain, weight],
        narrow,
        "summary",
        far=(0, 1, 2, 3, 4),
        scratch=[pltpu.VMEM((HEADS, TOK), F32), pltpu.SemaphoreType.DMA((5,))],
    )
    arrived = exchange(sent, "ctx")
    back = shape((TOK, HEAD_DIM), BF16)
    states, local, turned, columns, target_square = call(
        local_kernel,
        [back, full32, full16, shape((TOK, 128), F32), row],
        [arrived, queries, near_keys, near_values, target, cum],
        2 * wide,
        "local",
    )
    states = exchange(states.reshape(BLOCKS, 8, HEAD_DIM), "ctx").reshape(TOK, HEAD_DIM)
    attn, sums = call(
        output_kernel,
        [full32, shape((8, 4, TOK), F32)],
        [queries, states, local, columns, target, gain, target_square],
        narrow,
        "output",
    )
    sums = exchange(sums, "head")
    sent, grad_out = call(
        gradient_kernel,
        [slices, full16],
        [sums, attn, target, gain, weight, turned],
        narrow,
        "gradient",
        far_outs=(0,),
        scratch=[pltpu.VMEM(slices.shape, BF16), pltpu.SemaphoreType.DMA((HEADS,))],
    )
    arrived_back = exchange(sent, "ctx")
    grad_q, local_k, local_v, payoff, mark = call(
        local_gradient_kernel,
        [full16, full16, full16, row, shape((8, HEAD_DIM), F32)],
        [grad_out, queries, keys, values, states, cum, columns, sums],
        6 * wide,
        "local_gradient",
        far=(3,),
        scratch=[pltpu.VMEM((TOK, TOK), BF16), pltpu.SemaphoreType.DMA],
    )
    [later] = call(backward_scan_kernel, [back], [arrived_back, arrived, mark], 1000, "backward_scan")
    later = exchange(later.reshape(BLOCKS, 8, HEAD_DIM), "ctx").reshape(TOK, HEAD_DIM)
    grad_k, grad_v, gain_out = call(
        final_kernel,
        [full16, full16, shape((HEADS, HEAD_DIM), F32)],
        [later, keys, values, local_k, local_v, columns, arrived_back],
        2 * narrow,
        "final",
        far_outs=(0, 1, 2),
        scratch=pair[:2]
        + [pltpu.VMEM((HEADS, HEAD_DIM), F32), pltpu.SemaphoreType.DMA((2 * HEADS + 1,))],
    )
    return payoff.reshape(-1), grad_q, grad_k, grad_v, gain_out.reshape(-1)


def solution(mesh):
    placed = (
        P("ctx", "head"),
        P("ctx", "head"),
        P("ctx", "head"),
        P("head", "ctx"),
        P("ctx", "head"),
        P("head"),
        P("ctx"),
    )
    return jax.shard_map(
        local_part,
        mesh=mesh,
        in_specs=placed,
        out_specs=(P("ctx"), P("ctx", "head"), P("ctx", "head"), P("ctx", "head"), P("head")),
        check_vma=False,
    )
```
